512 devices in a mesh: seq: 128 (over y, z, core), chan: 4 (over x).
Axes of the slice: x: 4, y: 4, z: 16, core: 2. Of those that a mesh axis runs over, the one named last changes fastest.
Arguments:
- stream: bfloat16 [32768, 4096], P('seq', 'chan'), may hold values from -60 to 60
- norm_gain: float32 [4096], P('chan'), may hold values from 0.1 to 1.9
- gate_query: bfloat16 [32768, 4096], P('seq', 'chan'), may hold values from -6 to 6
- gate_key: bfloat16 [32768, 4096], P('seq', 'chan'), may hold values from -6 to 6
- gate_out: bfloat16 [32768, 4096], P('seq', 'chan'), may hold values from -6 to 6
- cotangent: bfloat16 [32768, 4096], P('seq', 'chan'), may hold values from -6 to 6
- medium_filter: float32 [128, 4096], P(None, 'chan'), may hold values from -0.53033009 to 0.53033009
- long_residue: float32 [4096], P('chan'), may hold values from 0.5 to 1.5
- long_rate: float32 [4096], P('chan'), may hold values from 9.1552734e-06 to 0.0333333333
Outputs:
- grad_query: bfloat16 [32768, 4096], P('seq', 'chan')
- grad_stream: bfloat16 [32768, 4096], P('seq', 'chan')
- grad_filter: float32 [128, 4096], P(None, 'chan')
- grad_residue: float32 [4096], P('chan')
The draws below stay inside these ranges and needn't reach their ends.
All inputs are finite; a program needn't handle non-finite values.
Results may differ from the reference program's by a relative error of at most 0.008.
Values sent between devices are 32-bit elements; how exact they have to be, the bound alone decides.
No kernel may reach another device: no remote copies, remote signals or barrier semaphores. Data moves between devices by JAX's collectives and lax.ppermute only.
A program may use at most 64 MiB of HBM per device.

```python
import math
import jax
import jax.numpy as jnp
from jax import lax

CHANNELS = 4096
FILTER_TAPS = 128
TOKENS = 32768


def region_field(key, lowest, highest):
    group_count = 16
    segment_rows = 16
    field = jnp.exp(jax.random.uniform(key, (TOKENS // segment_rows, 1, group_count, 1), jnp.float32, math.log(lowest), math.log(highest)))
    field = jnp.broadcast_to(field, (TOKENS // segment_rows, segment_rows, group_count, CHANNELS // group_count))
    return field.reshape(TOKENS, CHANNELS)


def make_stream(key):
    first_key = jax.random.fold_in(jax.random.fold_in(key, 101), 0)
    second_key = jax.random.fold_in(jax.random.fold_in(key, 101), 1)
    third_key = jax.random.fold_in(jax.random.fold_in(key, 101), 2)
    fifth_key = jax.random.fold_in(jax.random.fold_in(key, 101), 4)
    base = jnp.clip(jax.random.normal(first_key, (TOKENS, CHANNELS), jnp.float32), -4.0, 4.0)
    row_scale = jnp.exp(jax.random.uniform(second_key, (TOKENS, 1), jnp.float32, math.log(0.3), math.log(3.0)))
    jitter = jnp.exp(jax.random.uniform(third_key, (1, CHANNELS), jnp.float32, -0.3, 0.3))
    region = region_field(fifth_key, 0.3, 3.0)
    return base * row_scale * region * jitter


def draw_stream(key, part):
    return make_stream(key).astype(jnp.bfloat16)


def draw_gate_key(key, part):
    own_key = jax.random.fold_in(key, 202)
    magnitude = jnp.clip(jax.random.normal(own_key, (TOKENS, CHANNELS), jnp.float32), -6.0, 6.0)
    return magnitude.astype(jnp.bfloat16)


def positive_or_normal(key):
    values = jnp.clip(jax.random.normal(key, (TOKENS, CHANNELS), jnp.float32), -6.0, 6.0)
    return values


def draw_gate_query(key, part):
    return positive_or_normal(jax.random.fold_in(key, 303)).astype(jnp.bfloat16)


def draw_gate_out(key, part):
    return positive_or_normal(jax.random.fold_in(key, 404)).astype(jnp.bfloat16)


def draw_cotangent(key, part):
    noise_key = jax.random.fold_in(jax.random.fold_in(key, 505), 1)
    noise = jax.random.normal(noise_key, (TOKENS, CHANNELS), jnp.float32)
    values = jnp.clip(noise, -6.0, 6.0)
    return values.astype(jnp.bfloat16)


def draw_medium_filter(key, part):
    own_key = jax.random.fold_in(key, 606)
    spread = FILTER_TAPS ** (-0.5)
    values = jax.random.normal(own_key, (FILTER_TAPS, CHANNELS), jnp.float32)
    values = jnp.clip(values, -6.0, 6.0)
    return (values * spread).astype(jnp.float32)


def draw_long_rate(key, part):
    first_key, second_key = jax.random.split(key, 2)
    slow_flag = jax.random.randint(first_key, (CHANNELS,), 0, 2)
    fraction = jax.random.uniform(second_key, (CHANNELS,), jnp.float32)
    slow_rate = jnp.exp(math.log(0.3 / TOKENS) + fraction * math.log(2.0 / 0.3))
    fast_rate = jnp.exp(math.log(1.0 / 50.0) + fraction * math.log(50.0 / 30.0))
    return jnp.where(slow_flag == 1, slow_rate, fast_rate).astype(jnp.float32)


def block_levels(key, dims, shards, smallest, top_value):
    def one(position, parts):
        draws = jax.random.uniform(jax.random.fold_in(jax.random.fold_in(key, 6), position), (parts,), jnp.float32, smallest / len(shards), top_value / len(shards))
        return jnp.repeat(jnp.exp(draws), dims[position] // parts).reshape((-1,) + (1,) * (len(dims) - position - 1))

    gain = one(*shards[0])
    for cut in shards[1:]:
        gain = gain * one(*cut)
    return gain


def setup_inputs(seed: int = 0) -> dict:
    splits = jax.random.split(jax.random.key(seed), 10)
    return {
        "stream": draw_stream(jax.random.fold_in(splits[9], 71), 0),
        "norm_gain": jnp.clip(1.0 + 0.18 * jax.random.normal(splits[1], (CHANNELS,), jnp.float32), 0.1, 1.9),
        "gate_query": draw_gate_query(jax.random.fold_in(splits[9], 71), 0),
        "gate_key": draw_gate_key(jax.random.fold_in(splits[9], 71), 0),
        "gate_out": draw_gate_out(jax.random.fold_in(splits[9], 71), 0),
        "cotangent": draw_cotangent(jax.random.fold_in(splits[9], 71), 0),
        "medium_filter": draw_medium_filter(jax.random.fold_in(splits[9], 71), 0),
        "long_residue": jnp.clip(0.5 + 1.0 * jax.random.uniform(splits[7], (CHANNELS,), jnp.float32) ** block_levels(splits[7], (CHANNELS,), ((0, 4),), -0.2, 0.2), 0.5, 1.5),
        "long_rate": draw_long_rate(jax.random.fold_in(splits[9], 71), 0),
    }


EPSILON = 1e-05

def decayed_reverse(source, decay_row):

    def advance(carry, row_value):
        carry = decay_row * carry + row_value
        return (carry, carry)
    initial = jnp.zeros(source.shape[1:], jnp.float32)
    return lax.scan(advance, initial, source, reverse=True)[1]

def channel_block(operands):
    normed_block, query_block, key_block, outgate_block, cotan_block, filter_block, residue_block, rate_block = operands
    rim_width = FILTER_TAPS - 1
    block_width = normed_block.shape[1]
    product = key_block.astype(jnp.float32) * normed_block
    padded = jnp.concatenate([jnp.zeros((rim_width, block_width), jnp.float32), product], axis=0)

    def forward_tap(tap_index, running_sum):
        start = (rim_width - tap_index).astype(jnp.int32)
        shifted = lax.dynamic_slice_in_dim(padded, start, TOKENS, 0)
        return running_sum + filter_block[tap_index] * shifted
    mixed_rows = lax.fori_loop(0, FILTER_TAPS, forward_tap, jnp.zeros((TOKENS, block_width), jnp.float32))
    stored = (query_block.astype(jnp.float32) * mixed_rows).astype(jnp.bfloat16)
    normalizer = jnp.sqrt(-jnp.expm1(-2.0 * rate_block))
    grad_source = outgate_block.astype(jnp.float32) * cotan_block.astype(jnp.float32)
    reverse_state = decayed_reverse(grad_source, jnp.exp(-rate_block))
    grad_stored = residue_block * normalizer * reverse_state
    grad_query = (mixed_rows * grad_stored).astype(jnp.bfloat16)
    grad_mixed = query_block.astype(jnp.float32) * grad_stored
    trailing = jnp.concatenate([grad_mixed, jnp.zeros((rim_width, block_width), jnp.float32)], axis=0)

    def backward_tap(tap_index, running_sum):
        shifted = lax.dynamic_slice_in_dim(trailing, tap_index.astype(jnp.int32), TOKENS, 0)
        return running_sum + filter_block[tap_index] * shifted
    grad_product = lax.fori_loop(0, FILTER_TAPS, backward_tap, jnp.zeros((TOKENS, block_width), jnp.float32))
    grad_normed = key_block.astype(jnp.float32) * grad_product

    def filter_tap(tap_index):
        start = (rim_width - tap_index).astype(jnp.int32)
        shifted = lax.dynamic_slice_in_dim(padded, start, TOKENS, 0)
        return lax.optimization_barrier(jnp.sum(grad_mixed * shifted, axis=0))
    grad_scale = TOKENS ** (-0.5)
    grad_filter = lax.map(filter_tap, jnp.arange(FILTER_TAPS, dtype=jnp.int32)) * grad_scale
    grad_residue = normalizer * lax.optimization_barrier(jnp.sum(stored.astype(jnp.float32) * reverse_state, axis=0)) * grad_scale
    return (grad_query, grad_normed, grad_filter, grad_residue)

def reference(stream, norm_gain, gate_query, gate_key, gate_out, cotangent, medium_filter, long_residue, long_rate):
    inputs = stream.astype(jnp.float32)
    inv_rms = lax.rsqrt(lax.optimization_barrier(jnp.mean(inputs * inputs, axis=1, keepdims=True)) + EPSILON)
    normed = inputs * inv_rms * norm_gain
    block_width = math.gcd(CHANNELS, 256)
    block_count = CHANNELS // block_width

    def split_cols(matrix):
        return jnp.moveaxis(matrix.reshape(matrix.shape[0], block_count, block_width), 1, 0)

    def join_cols(stack):
        return jnp.moveaxis(stack, 0, 1).reshape(stack.shape[1], CHANNELS)
    results = lax.map(channel_block, (split_cols(normed), split_cols(gate_query), split_cols(gate_key), split_cols(gate_out), split_cols(cotangent), split_cols(medium_filter), long_residue.reshape(block_count, block_width), long_rate.reshape(block_count, block_width)))
    grad_query = join_cols(results[0])
    grad_normed = join_cols(results[1])
    grad_filter = join_cols(results[2])
    grad_residue = results[3].reshape(CHANNELS)
    weighted = norm_gain * grad_normed
    row_dots = lax.optimization_barrier(jnp.mean(weighted * inputs, axis=1, keepdims=True))
    grad_stream = (inv_rms * (weighted - inputs * inv_rms * inv_rms * row_dots)).astype(jnp.bfloat16)
    return (grad_query, grad_stream, grad_filter, grad_residue)
```

```python
import jax
import jax.numpy as jnp
import numpy as np
from jax import lax
from jax.experimental import pallas as pl
from jax.experimental.pallas import tpu as pltpu
from jax.sharding import Mesh, PartitionSpec as P

EPSILON = 1e-05
ROWS = 256
TAPS = 128
CHANS = 1024
TOKENS = 32768
CHANNEL_TOTAL = 4096
LANES = 128
TILES = CHANS // LANES
POINTS = ROWS + TAPS
HALF = POINTS // 2
Y, Z = (4, 16)
PLANE = Y * Z
F32 = jnp.float32
BF16 = jnp.bfloat16


def transform_tables():
    k = np.arange(HALF, dtype=np.int64)[:, None]
    n = np.arange(POINTS, dtype=np.int64)[None, :]
    angle = np.pi * (((2 * k + 1) * n) % (2 * POINTS)).astype(np.float64) / POINTS
    table = np.concatenate([np.cos(angle), -np.sin(angle)], axis=0)
    forward = table.astype(BF16)
    inverse = np.ascontiguousarray(table.T).astype(BF16)
    lags = np.ascontiguousarray(table.T[TAPS:0:-1]).astype(BF16)
    return forward, inverse, lags


def call(kernel, outs, *args, specs=None, flops=0):
    vmem = pl.BlockSpec(memory_space=pltpu.VMEM)
    sizes = [a.size * a.dtype.itemsize for a in args]
    sizes += [int(np.prod(o.shape)) * o.dtype.itemsize for o in outs]
    result = pl.pallas_call(
        kernel,
        out_shape=tuple(outs),
        in_specs=[vmem] * len(args) if specs is None else specs,
        out_specs=tuple([vmem] * len(outs)),
        compiler_params=pltpu.CompilerParams(vmem_limit_bytes=40 * 1024 * 1024),
        cost_estimate=pl.CostEstimate(
            flops=flops, bytes_accessed=sum(sizes), transcendentals=0
        ),
    )(*args)
    return result


def shape(dims, dtype=F32):
    return jax.ShapeDtypeStruct(dims, dtype)


SMEM = pl.BlockSpec(memory_space=pltpu.SMEM)
VMEM = pl.BlockSpec(memory_space=pltpu.VMEM)


def dot(a, b):
    return lax.dot_general(
        a, b, (((1,), (0,)), ((), ())), preferred_element_type=F32
    )


def lane_tile(tile):
    return slice(tile * LANES, (tile + 1) * LANES)


def row_scale(total):
    inv = lax.rsqrt(total / CHANNEL_TOTAL + EPSILON)
    return jnp.broadcast_to(inv, (LANES, ROWS)).T


def head_kernel(out_ref, cot_ref, rate_ref, first_ref):
    rank = lax.broadcasted_iota(jnp.int32, (8, LANES), 0).astype(F32)
    for tile in range(TILES):
        cols = lane_tile(tile)
        rate = rate_ref[tile : tile + 1, :]
        source = out_ref[:, cols].astype(F32) * cot_ref[:, cols].astype(F32)
        eight = jnp.exp(-8.0 * rate)
        total = source[ROWS - 8 :, :]
        for group in range(ROWS // 8 - 2, -1, -1):
            total = total * eight + source[group * 8 : group * 8 + 8, :]
        total = total * jnp.exp(-rate * rank)
        first_ref[tile : tile + 1, :] = jnp.sum(total, axis=0, keepdims=True)


def pair_kernel(core_ref, own_ref, other_ref, rate_ref, spread_ref):
    decay = jnp.exp(-ROWS * rate_ref[...])
    own, other = (own_ref[...], other_ref[...])
    is_first = core_ref[0] == 0
    low = jnp.where(is_first, own, other)
    high = jnp.where(is_first, other, own)
    spread_ref[...] = jnp.broadcast_to(low + decay * high, spread_ref.shape)


def squares_kernel(stream_ref, total_ref):
    acc = jnp.zeros((ROWS, LANES), F32)
    for tile in range(TILES):
        value = stream_ref[:, lane_tile(tile)].astype(F32)
        acc = acc + value * value
    total_ref[...] = jnp.sum(acc.T, axis=0, keepdims=True)


def product_kernel(total_ref, stream_ref, key_ref, gain_ref, product_ref, rim_ref):
    inv = row_scale(total_ref[...])
    for tile in range(TILES):
        cols = lane_tile(tile)
        normed = stream_ref[:, cols].astype(F32) * inv * gain_ref[tile : tile + 1, :]
        product = key_ref[:, cols].astype(F32) * normed
        product_ref[:, cols] = product.astype(BF16)
        rim_ref[:, cols] = product[ROWS - TAPS :, :]


def scan_kernel(out_ref, cot_ref, rate_ref, local_ref):
    rank = lax.broadcasted_iota(jnp.int32, (8, LANES), 0)
    for tile in range(TILES):
        cols = lane_tile(tile)
        rate = rate_ref[tile : tile + 1, :]
        source = out_ref[:, cols].astype(F32) * cot_ref[:, cols].astype(F32)
        coefs = [
            (s, jnp.where(rank < 8 - s, jnp.exp(-float(s) * rate), 0.0)) for s in (1, 2, 4)
        ]
        power = jnp.exp(-rate * (8 - rank).astype(F32))
        carry = jnp.zeros((1, LANES), F32)
        for group in range(ROWS // 8 - 1, -1, -1):
            value = source[group * 8 : group * 8 + 8, :]
            for s, coef in coefs:
                value = value + coef * pltpu.roll(value, 8 - s, 0)
            value = value + power * carry
            local_ref[group * 8 : group * 8 + 8, cols] = value
            carry = value[0:1, :]


def mul_conj(a, b):
    ar, ai = (a[:HALF], a[HALF:])
    br, bi = (b[:HALF], b[HALF:])
    return jnp.concatenate([ar * br + ai * bi, ar * bi - ai * br], axis=0).astype(BF16)


def mul(a, b):
    ar, ai = (a[:HALF], a[HALF:])
    br, bi = (b[:HALF], b[HALF:])
    return jnp.concatenate([ar * br - ai * bi, ar * bi + ai * br], axis=0).astype(BF16)


def tail_decay(rate):
    rows = lax.broadcasted_iota(jnp.int32, (8, LANES), 0)
    power = jnp.exp(-rate * (8 - rows).astype(F32))
    groups = []
    for group in range(ROWS // 8):
        groups.append(power * jnp.exp(-rate * float(ROWS - 8 - 8 * group)))
    return jnp.concatenate(groups, axis=0)


def filter_kernel(
    fwd_ref, lag_ref, product_ref, rim_ref, local_ref, query_ref, rate_ref, residue_ref, a_ref, b_ref
):
    for tile in range(TILES):
        cols = lane_tile(tile)
        rate = rate_ref[tile : tile + 1, :]
        scale = residue_ref[tile : tile + 1, :]
        ext = jnp.concatenate([rim_ref[:, cols].astype(BF16), product_ref[:, cols]], axis=0)
        product = dot(fwd_ref[...], ext)
        query = query_ref[:, cols].astype(F32) * scale
        first = (query * local_ref[:, cols]).astype(BF16)
        second = (query * tail_decay(rate)).astype(BF16)
        for part, ref in ((first, a_ref), (second, b_ref)):
            spectrum = dot(fwd_ref[:, :ROWS], part)
            taps = dot(lag_ref[...], mul_conj(spectrum, product))
            for group in range(TAPS // 8):
                ref[group * TILES + tile] = taps[group * 8 : group * 8 + 8, :]


def carry_kernel(place_ref, pairs_ref, own_ref, other_ref, rate_ref, carry_ref):
    chip, core = (place_ref[0], place_ref[1])
    rate = rate_ref[...]
    carry = jnp.zeros_like(rate)
    for later in range(1, PLANE):
        gap = later - chip - 1
        weight = jnp.exp(-rate * (2.0 * ROWS) * jnp.maximum(gap, 0).astype(F32))
        carry = carry + jnp.where(gap >= 0, weight, 0.0) * pairs_ref[later]
    below = other_ref[...] + jnp.exp(-ROWS * rate) * carry
    carry_ref[...] = jnp.where(core == 0, below, carry)


def join_kernel(core_ref, carry_ref, a_ref, b_ref, keep_ref, send_ref):
    carry = carry_ref[...]
    count = keep_ref.shape[0]
    mine = core_ref[0] * count
    theirs = count - mine
    for group in range(count // TILES):
        for tile in range(TILES):
            at = group * TILES + tile
            row = carry[tile : tile + 1, :]
            send_ref[at] = a_ref[theirs + at] + row * b_ref[theirs + at]
            keep_ref[at] = a_ref[mine + at] + row * b_ref[mine + at]


def add_kernel(a_ref, b_ref, out_ref):
    out_ref[...] = a_ref[...] + b_ref[...]


def spread_sum_kernel(parts_ref, spread_ref):
    total = jnp.sum(parts_ref[...], axis=0)
    spread_ref[...] = jnp.broadcast_to(total, spread_ref.shape)


def finish_kernel(core_ref, own_ref, other_ref, filter_ref, residue_ref, filter_out, residue_out):
    scale = TOKENS ** (-0.5) * 2.0 / POINTS
    count = own_ref.shape[0]
    is_first = core_ref[0] == 0
    for tile in range(TILES):
        cols = lane_tile(tile)
        total = jnp.zeros((8, LANES), F32)
        for group in range(TAPS // 8):
            at = (group * TILES + tile) % count
            low = group * TILES + tile < count
            own, other = (own_ref[at], other_ref[at])
            value = jnp.where(is_first, own, other) if low else jnp.where(is_first, other, own)
            value = value * scale
            rows = slice(group * 8, group * 8 + 8)
            filter_out[rows, cols] = value
            total = total + filter_ref[rows, cols] * value
        total = jnp.sum(total, axis=0, keepdims=True)
        residue_out[tile : tile + 1, :] = total / residue_ref[tile : tile + 1, :]


def query_kernel(
    fwd_ref, inv_ref, product_ref, rim_ref, local_ref, carry_ref, query_ref, filter_ref, rate_ref,
    scale_ref, grad_ref, mixed_grad_ref, head_ref,
):
    for tile in range(TILES):
        cols = lane_tile(tile)
        rate = rate_ref[tile : tile + 1, :]
        ext = jnp.concatenate([rim_ref[:, cols].astype(BF16), product_ref[:, cols]], axis=0)
        product = dot(fwd_ref[...], ext)
        taps = dot(fwd_ref[:, :TAPS], filter_ref[:, cols].astype(BF16))
        mixed = dot(inv_ref[TAPS:, :], mul(product, taps)) * (2.0 / POINTS)
        state = local_ref[:, cols] + tail_decay(rate) * carry_ref[tile : tile + 1, :]
        stored = state * scale_ref[tile : tile + 1, :]
        grad_ref[:, cols] = (mixed * stored).astype(BF16)
        grad_mixed = query_ref[:, cols].astype(F32) * stored
        mixed_grad_ref[:, cols] = grad_mixed.astype(BF16)
        head_ref[:, cols] = grad_mixed[:TAPS]


def weighted_kernel(
    fwd_ref, inv_ref, grad_ref, after_ref, filter_ref, key_ref, stream_ref, gain_ref, weighted_ref, dots_ref
):
    acc = jnp.zeros((ROWS, LANES), F32)
    for tile in range(TILES):
        cols = lane_tile(tile)
        ext = jnp.concatenate([grad_ref[:, cols], after_ref[:, cols].astype(BF16)], axis=0)
        grad = dot(fwd_ref[...], ext)
        taps = dot(fwd_ref[:, :TAPS], filter_ref[:, cols].astype(BF16))
        back = dot(inv_ref[:ROWS, :], mul_conj(taps, grad)) * (2.0 / POINTS)
        weighted = gain_ref[tile : tile + 1, :] * key_ref[:, cols].astype(F32) * back
        weighted_ref[:, cols] = weighted
        acc = acc + weighted * stream_ref[:, cols].astype(F32)
    dots_ref[...] = jnp.sum(acc.T, axis=0, keepdims=True)


def stream_kernel(total_ref, dots_ref, weighted_ref, stream_ref, out_ref):
    inv = row_scale(total_ref[...])
    dots = jnp.broadcast_to(dots_ref[...] / CHANNEL_TOTAL, (LANES, ROWS)).T
    factor = inv * inv * dots
    for tile in range(TILES):
        cols = lane_tile(tile)
        value = weighted_ref[:, cols] - stream_ref[:, cols].astype(F32) * factor
        out_ref[:, cols] = (inv * value).astype(BF16)


def body(
    stream, norm_gain, gate_query, gate_key, gate_out, cotangent, medium_filter, long_residue, long_rate
):
    forward, inverse, lags = (jnp.asarray(t) for t in transform_tables())
    gain = norm_gain.reshape(TILES, LANES)
    rate = long_rate.reshape(TILES, LANES)
    residue = long_residue.reshape(TILES, LANES)
    scale = residue * jnp.sqrt(-jnp.expm1(-2.0 * rate))
    core = lax.axis_index("core").astype(jnp.int32)
    chip = (lax.axis_index("y") * Z + lax.axis_index("z")).astype(jnp.int32)
    core_at = core.reshape(1)
    place = jnp.stack([chip, core])
    plane = ("y", "z")
    seq = ("y", "z", "core")
    swap = [(0, 1), (1, 0)]
    dense = (TILES, LANES)
    full = (ROWS, CHANS)

    (first,) = call(head_kernel, [shape(dense)], gate_out, cotangent, rate)
    other = lax.ppermute(first, "core", swap)
    (spread,) = call(
        pair_kernel, [shape((PLANE,) + dense)], core_at, first, other, rate, specs=[SMEM, VMEM, VMEM, VMEM]
    )
    pairs = lax.all_to_all(spread, plane, 0, 0, tiled=True)

    (squares,) = call(squares_kernel, [shape((1, ROWS))], stream)
    squares = lax.psum(squares, "chan")
    product, rim = call(
        product_kernel, [shape(full, BF16), shape((TAPS, CHANS))], squares, stream, gate_key, gain
    )
    count = 2 * PLANE
    before = lax.ppermute(rim, seq, [(i, i + 1) for i in range(count - 1)])
    (local,) = call(scan_kernel, [shape(full)], gate_out, cotangent, rate)
    tiles = (TAPS // 8 * TILES, 8, LANES)
    part_a, part_b = call(
        filter_kernel, [shape(tiles), shape(tiles)], forward, lags, product, before, local, gate_query,
        rate, scale, flops=2 * CHANS * POINTS * (POINTS + 2 * ROWS + 2 * TAPS),
    )

    (carry,) = call(
        carry_kernel, [shape(dense)], place, pairs, first, other, rate, specs=[SMEM] + [VMEM] * 4
    )

    half = (tiles[0] // 2, 8, LANES)
    keep, send = call(
        join_kernel, [shape(half), shape(half)], core_at, carry, part_a, part_b, specs=[SMEM] + [VMEM] * 3
    )
    got = lax.ppermute(send, "core", swap)
    (chip_sum,) = call(add_kernel, [shape(half)], keep, got)
    parts = lax.all_to_all(chip_sum, plane, 0, 0, tiled=True)
    (spread_sum,) = call(spread_sum_kernel, [shape(half)], parts)
    own_half = lax.all_to_all(spread_sum, plane, 0, 0, tiled=True)
    other_half = lax.ppermute(own_half, "core", swap)
    grad_filter, grad_residue = call(
        finish_kernel, [shape((TAPS, CHANS)), shape(dense)], core_at, own_half, other_half, medium_filter,
        residue, specs=[SMEM] + [VMEM] * 4,
    )

    grad_query, grad_mixed, head = call(
        query_kernel, [shape(full, BF16), shape(full, BF16), shape((TAPS, CHANS))], forward, inverse, product,
        before, local, carry, gate_query, medium_filter, rate, scale,
        flops=2 * CHANS * POINTS * (POINTS + ROWS + TAPS),
    )
    after = lax.ppermute(head, seq, [(i + 1, i) for i in range(count - 1)])
    weighted, dots = call(
        weighted_kernel, [shape(full), shape((1, ROWS))], forward, inverse, grad_mixed, after, medium_filter,
        gate_key, stream, gain, flops=2 * CHANS * POINTS * (POINTS + ROWS + TAPS),
    )
    dots = lax.psum(dots, "chan")
    (grad_stream,) = call(stream_kernel, [shape(full, BF16)], squares, dots, weighted, stream)
    return (grad_query, grad_stream, grad_filter, grad_residue.reshape(CHANS))


def solution(mesh):
    devices = mesh.devices.reshape(Y, Z, 2, mesh.devices.shape[1])
    fine = Mesh(devices, ("y", "z", "core", "chan"))
    seq = ("y", "z", "core")
    rows, chans = (P(seq, "chan"), P("chan"))
    in_specs = (rows, chans, rows, rows, rows, rows, P(None, "chan"), chans, chans)
    out_specs = (rows, rows, P(None, "chan"), chans)
    return jax.shard_map(body, mesh=fine, in_specs=in_specs, out_specs=out_specs, check_vma=False)
```

```python
import jax
import jax.numpy as jnp
import numpy as np
from jax import lax
from jax.experimental import pallas as pl
from jax.experimental.pallas import tpu as pltpu
from jax.sharding import Mesh, PartitionSpec as P

EPSILON = 1e-05
ROWS = 256
TAPS = 128
CHANS = 1024
TOKENS = 32768
CHANNEL_TOTAL = 4096
LANES = 128
TILES = CHANS // LANES
WIDTH = 256
PER = WIDTH // LANES
STEPS = CHANS // WIDTH
GROUPS = TAPS // 8
POINTS = ROWS + TAPS
HALF = POINTS // 2
X, Y, Z, ZL = (4, 4, 16, 4)
ZH = Z // ZL
PLANE = Y * Z
LARGE = 60 * 1024 * 1024
SMALL = 8 * 1024 * 1024
F32 = jnp.float32
BF16 = jnp.bfloat16
DENSE = (TILES, LANES)
FULL = (ROWS, CHANS)


def transform_tables():
    k = np.arange(HALF, dtype=np.int64)[:, None]
    n = np.arange(POINTS, dtype=np.int64)[None, :]
    angle = np.pi * (((2 * k + 1) * n) % (2 * POINTS)).astype(np.float64) / POINTS
    table = np.concatenate([np.cos(angle), -np.sin(angle)], axis=0)
    forward = table.astype(BF16)
    inverse = np.ascontiguousarray(table.T).astype(BF16)
    lags = np.ascontiguousarray(table.T[TAPS:0:-1]).astype(BF16)
    return forward, inverse, lags


SMEM = pl.BlockSpec(memory_space=pltpu.SMEM)
VMEM = pl.BlockSpec(memory_space=pltpu.VMEM)


def shape(dims, dtype=F32):
    return jax.ShapeDtypeStruct(dims, dtype)


def cols(rows):
    return pl.BlockSpec((rows, WIDTH), lambda j: (0, j))


def whole(*dims):
    return pl.BlockSpec(dims, lambda j: (0,) * len(dims))


def cost(args, outs, flops):
    sizes = [a.size * a.dtype.itemsize for a in args]
    sizes += [int(np.prod(o.shape)) * o.dtype.itemsize for o in outs]
    return pl.CostEstimate(flops=flops, bytes_accessed=sum(sizes), transcendentals=0)


def small(kernel, outs, *args, specs=None):
    return pl.pallas_call(
        kernel,
        out_shape=tuple(outs),
        in_specs=[VMEM] * len(args) if specs is None else specs,
        out_specs=tuple([VMEM] * len(outs)),
        compiler_params=pltpu.CompilerParams(vmem_limit_bytes=SMALL),
        cost_estimate=cost(args, outs, 0),
    )(*args)


def large(kernel, outs, out_specs, args, in_specs, scratch=(), flops=0):
    return pl.pallas_call(
        kernel,
        grid=(STEPS,),
        out_shape=tuple(outs),
        in_specs=in_specs,
        out_specs=tuple(out_specs),
        scratch_shapes=list(scratch),
        compiler_params=pltpu.CompilerParams(vmem_limit_bytes=LARGE),
        cost_estimate=cost(args, outs, flops),
    )(*args)


def dot(a, b):
    return lax.dot_general(
        a, b, (((1,), (0,)), ((), ())), preferred_element_type=F32
    )


def row(ref):
    at = pl.program_id(0) * PER
    return jnp.concatenate([ref[pl.ds(at + i, 1), :] for i in range(PER)], axis=1)


def put_row(ref, value):
    at = pl.program_id(0) * PER
    for i in range(PER):
        ref[pl.ds(at + i, 1), :] = value[:, i * LANES : (i + 1) * LANES]


def fold(value):
    return sum(value[:, i * LANES : (i + 1) * LANES] for i in range(PER))


def row_mean(parts_ref):
    packed = jnp.sum(parts_ref[...], axis=0) / CHANNEL_TOTAL
    return jnp.concatenate(
        [jnp.broadcast_to(packed[i : i + 1], (LANES, LANES)).T for i in range(ROWS // LANES)], axis=0
    )


def widen(value):
    return jnp.concatenate([value] * PER, axis=1)


def spread_rows(acc, out_ref):
    total = jnp.sum(acc.T, axis=0, keepdims=True)
    packed = jnp.concatenate([total[:, :LANES], total[:, LANES:], jnp.zeros((6, LANES), F32)], axis=0)
    out_ref[...] = jnp.broadcast_to(packed, out_ref.shape)


def start_kernel(stream_ref, out_ref, cot_ref, rate_ref, squares_ref, spread_ref, local_ref, acc_ref, first_ref):
    step = pl.program_id(0)
    value = stream_ref[...].astype(F32)
    squares = fold(value * value)

    @pl.when(step == 0)
    def _():
        acc_ref[...] = squares

    @pl.when(step > 0)
    def _():
        acc_ref[...] += squares

    rank = lax.broadcasted_iota(jnp.int32, (8, WIDTH), 0)
    rate = row(rate_ref)
    source = out_ref[...].astype(F32) * cot_ref[...].astype(F32)
    coefs = [(s, jnp.where(rank < 8 - s, jnp.exp(-float(s) * rate), 0.0)) for s in (1, 2, 4)]
    power = jnp.exp(-rate * (8 - rank).astype(F32))
    carry = jnp.zeros((1, WIDTH), F32)
    for group in range(ROWS // 8 - 1, -1, -1):
        value = source[group * 8 : group * 8 + 8, :]
        for s, coef in coefs:
            value = value + coef * pltpu.roll(value, 8 - s, 0)
        value = value + power * carry
        local_ref[group * 8 : group * 8 + 8, :] = value
        carry = value[0:1, :]
    put_row(first_ref, carry)

    @pl.when(step == STEPS - 1)
    def _():
        spread_rows(acc_ref[...], squares_ref)
        spread_ref[...] = jnp.broadcast_to(first_ref[...], spread_ref.shape)


def column_kernel(place_ref, parts_ref, first_ref, rate_ref, out_ref):
    z = place_ref[1]
    pace = rate_ref[...] * (-2.0 * ROWS)
    ahead = jnp.zeros(DENSE, F32)
    total = jnp.zeros(DENSE, F32)
    for other in range(Z):
        value = parts_ref[other]
        gap = other - z - 1
        weight = jnp.exp(pace * jnp.maximum(gap, 0).astype(F32))
        ahead = ahead + jnp.where(gap >= 0, weight, 0.0) * value
        total = total + jnp.exp(pace * float(other)) * value
    count = out_ref.shape[0]
    out_ref[:, 0] = jnp.broadcast_to(total, (count,) + DENSE)
    out_ref[:, 1] = jnp.broadcast_to(ahead, (count,) + DENSE)
    out_ref[:, 2] = jnp.broadcast_to(first_ref[0], (count,) + DENSE)


def carry_kernel(place_ref, parts_ref, rate_ref, carry_ref):
    y, z, core = (place_ref[0], place_ref[1], place_ref[2])
    rate = rate_ref[...]
    decay = jnp.exp(-ROWS * rate)
    rest = jnp.exp(rate * (-2.0 * ROWS) * (Z - 1 - z).astype(F32))
    both = []
    for parity in range(2):
        planes = jnp.zeros(DENSE, F32)
        for later in range(1, Y):
            gap = later - y - 1
            weight = jnp.exp(rate * (-2.0 * ROWS * Z) * jnp.maximum(gap, 0).astype(F32))
            planes = planes + jnp.where(gap >= 0, weight, 0.0) * parts_ref[later * 2 + parity, 0]
        both.append(parts_ref[y * 2 + parity, 1] + rest * planes)
    last = both[0] + decay * both[1]
    carry_ref[...] = jnp.where(core == 0, parts_ref[y * 2 + 1, 2] + decay * last, last)


def norm_kernel(total_ref, after_ref, inv_ref):
    inv_ref[...] = lax.rsqrt(row_mean(total_ref) + EPSILON)


def product_kernel(inv_ref, stream_ref, key_ref, gain_ref, product_ref, rim_ref):
    normed = stream_ref[...].astype(F32) * widen(inv_ref[...]) * row(gain_ref)
    product = key_ref[...].astype(F32) * normed
    product_ref[...] = product.astype(BF16)
    rim_ref[...] = product[ROWS - TAPS :, :]


def mul_conj(a, b):
    ar, ai = (a[:HALF], a[HALF:])
    br, bi = (b[:HALF], b[HALF:])
    return jnp.concatenate([ar * br + ai * bi, ar * bi - ai * br], axis=0).astype(BF16)


def mul(a, b):
    ar, ai = (a[:HALF], a[HALF:])
    br, bi = (b[:HALF], b[HALF:])
    return jnp.concatenate([ar * br - ai * bi, ar * bi + ai * br], axis=0).astype(BF16)


def grad_stored(local_ref, rate_ref, scale_ref, carry_ref):
    rate = row(rate_ref)
    rank = lax.broadcasted_iota(jnp.int32, (8, WIDTH), 0)
    power = jnp.exp(-rate * (8 - rank).astype(F32)) * row(carry_ref)
    groups = []
    for group in range(ROWS // 8):
        far = power * jnp.exp(-rate * float(ROWS - 8 - 8 * group))
        groups.append(local_ref[group * 8 : group * 8 + 8, :] + far)
    return jnp.concatenate(groups, axis=0) * row(scale_ref)


def filter_kernel(
    place_ref, fwd_ref, lag_ref, product_ref, rim_ref, local_ref, query_ref, rate_ref, scale_ref, carry_ref,
    keep_ref, send_ref, mixed_grad_ref, head_ref,
):
    ext = jnp.concatenate([rim_ref[...].astype(BF16), product_ref[...]], axis=0)
    product = dot(fwd_ref[...], ext)
    grad_mixed = query_ref[...].astype(F32) * grad_stored(local_ref, rate_ref, scale_ref, carry_ref)
    head_ref[...] = grad_mixed[:TAPS]
    grad_mixed = grad_mixed.astype(BF16)
    mixed_grad_ref[...] = grad_mixed
    spectrum = dot(fwd_ref[:, :ROWS], grad_mixed)
    taps = dot(lag_ref[...], mul_conj(spectrum, product))
    is_first = place_ref[2] == 0
    for group in range(GROUPS // 2):
        low = taps[group * 8 : group * 8 + 8, :]
        high = taps[TAPS // 2 + group * 8 : TAPS // 2 + group * 8 + 8, :]
        keep = jnp.where(is_first, low, high)
        send = jnp.where(is_first, high, low)
        for i in range(PER):
            keep_ref[group, i] = keep[:, i * LANES : (i + 1) * LANES]
            send_ref[group, i] = send[:, i * LANES : (i + 1) * LANES]


def query_kernel(
    fwd_ref, inv_ref, product_ref, rim_ref, local_ref, filter_ref, rate_ref, scale_ref, carry_ref, grad_ref, token_ref
):
    ext = jnp.concatenate([rim_ref[...].astype(BF16), product_ref[...]], axis=0)
    product = dot(fwd_ref[...], ext)
    taps = dot(fwd_ref[:, :TAPS], filter_ref[...].astype(BF16))
    mixed = dot(inv_ref[TAPS:, :], mul(product, taps)) * (2.0 / POINTS)
    grad_ref[...] = (mixed * grad_stored(local_ref, rate_ref, scale_ref, carry_ref)).astype(BF16)
    token_ref[...] = carry_ref[...]


def weighted_kernel(
    fwd_ref, inv_ref, grad_ref, after_ref, filter_ref, key_ref, stream_ref, gain_ref, weighted_ref, dots_ref, acc_ref
):
    step = pl.program_id(0)
    ext = jnp.concatenate([grad_ref[...], after_ref[...].astype(BF16)], axis=0)
    grad = dot(fwd_ref[...], ext)
    taps = dot(fwd_ref[:, :TAPS], filter_ref[...].astype(BF16))
    back = dot(inv_ref[:ROWS, :], mul_conj(taps, grad)) * (2.0 / POINTS)
    weighted = row(gain_ref) * key_ref[...].astype(F32) * back
    weighted_ref[...] = weighted
    dots = fold(weighted * stream_ref[...].astype(F32))

    @pl.when(step == 0)
    def _():
        acc_ref[...] = dots

    @pl.when(step > 0)
    def _():
        acc_ref[...] += dots

    @pl.when(step == STEPS - 1)
    def _():
        spread_rows(acc_ref[...], dots_ref)


def stream_kernel(inv_ref, dots_ref, weighted_ref, stream_ref, out_ref, token_ref, factor_ref):
    inv = inv_ref[...]

    @pl.when(pl.program_id(0) == 0)
    def _():
        factor_ref[...] = inv * inv * row_mean(dots_ref)

    value = weighted_ref[...] - stream_ref[...].astype(F32) * widen(factor_ref[...])
    out_ref[...] = (widen(inv) * value).astype(BF16)
    token_ref[...] = factor_ref[0:8, :]


def add_kernel(a_ref, b_ref, out_ref):
    out_ref[...] = a_ref[...] + b_ref[...]


def spread_sum_kernel(parts_ref, after_ref, spread_ref):
    total = jnp.sum(parts_ref[...], axis=0)
    spread_ref[...] = jnp.broadcast_to(total, spread_ref.shape)


def fence_kernel(value_ref, after_ref, out_ref):
    out_ref[...] = value_ref[...]


def finish_kernel(place_ref, own_ref, other_ref, filter_ref, residue_ref, filter_out, residue_out):
    scale = TOKENS ** (-0.5) * 2.0 / POINTS
    count = own_ref.shape[0]
    is_first = place_ref[2] == 0
    for tile in range(TILES):
        lanes = slice(tile * LANES, (tile + 1) * LANES)
        total = jnp.zeros((8, LANES), F32)
        for group in range(GROUPS):
            at = (group * TILES + tile) % count
            low = group * TILES + tile < count
            own, other = (own_ref[at], other_ref[at])
            value = jnp.where(is_first, own, other) if low else jnp.where(is_first, other, own)
            value = value * scale
            rows = slice(group * 8, group * 8 + 8)
            filter_out[rows, lanes] = value
            total = total + filter_ref[rows, lanes] * value
        total = jnp.sum(total, axis=0, keepdims=True)
        residue_out[tile : tile + 1, :] = total / residue_ref[tile : tile + 1, :]


def body(
    stream, norm_gain, gate_query, gate_key, gate_out, cotangent, medium_filter, long_residue, long_rate
):
    forward, inverse, lags = (jnp.asarray(t) for t in transform_tables())
    gain, rate, residue = (v.reshape(DENSE) for v in (norm_gain, long_rate, long_residue))
    scale = residue * jnp.sqrt(-jnp.expm1(-2.0 * rate))
    z_at = lax.axis_index(("zh", "zl"))
    place = jnp.stack([lax.axis_index("y"), z_at, lax.axis_index("core")]).astype(jnp.int32)
    swap = [(0, 1), (1, 0)]
    seq = ("y", "zh", "zl", "core")
    count = 2 * PLANE
    dense, table = (whole(*DENSE), whole(POINTS, POINTS))

    shares = (X,) + DENSE
    squares, spread, local = large(
        start_kernel, [shape(shares), shape((Z,) + DENSE), shape(FULL)],
        [whole(*shares), whole(Z, *DENSE), cols(ROWS)],
        (stream, gate_out, cotangent, rate), [cols(ROWS)] * 3 + [dense],
        scratch=[pltpu.VMEM((ROWS, LANES), F32), pltpu.VMEM(DENSE, F32)],
    )
    squares = lax.all_to_all(squares, "chan", 0, 0, tiled=True)
    column = lax.all_to_all(spread, ("zh", "zl"), 0, 0, tiled=True)
    thin = whole(ROWS, LANES)
    (inv,) = small(norm_kernel, [shape((ROWS, LANES))], squares, column)
    product, rim = large(
        product_kernel, [shape(FULL, BF16), shape((TAPS, CHANS))], [cols(ROWS), cols(TAPS)],
        (inv, stream, gate_key, gain), [thin, cols(ROWS), cols(ROWS), dense],
    )
    before = lax.ppermute(rim, seq, [(i, i + 1) for i in range(count - 1)])
    (sums,) = small(
        column_kernel, [shape((2 * Y, 3) + DENSE)], place, column, spread, rate, specs=[SMEM] + [VMEM] * 3
    )
    sums = lax.all_to_all(sums, ("y", "core"), 0, 0, tiled=True)
    (carry,) = small(carry_kernel, [shape(DENSE)], place, sums, rate, specs=[SMEM] + [VMEM] * 2)

    half = (GROUPS // 2, TILES, 8, LANES)
    blocks = pl.BlockSpec((GROUPS // 2, PER, 8, LANES), lambda j: (0, j, 0, 0))
    keep, send, grad_mixed, head = large(
        filter_kernel, [shape(half), shape(half), shape(FULL, BF16), shape((TAPS, CHANS))],
        [blocks, blocks, cols(ROWS), cols(TAPS)],
        (place, forward, lags, product, before, local, gate_query, rate, scale, carry),
        [SMEM, table, whole(TAPS, POINTS), cols(ROWS), cols(TAPS), cols(ROWS), cols(ROWS), dense, dense, dense],
        flops=2 * CHANS * POINTS * (POINTS + ROWS + TAPS),
    )

    got = lax.ppermute(send, "core", swap)
    (chip_sum,) = small(add_kernel, [shape(half)], keep, got)
    after = lax.ppermute(head, seq, [(i + 1, i) for i in range(count - 1)])
    parts = lax.all_to_all(chip_sum.reshape(PLANE, 8, LANES), ("y", "zl"), 0, 0, tiled=True)
    grad_query, token = large(
        query_kernel, [shape(FULL, BF16), shape(DENSE)], [cols(ROWS), dense],
        (forward, inverse, product, before, local, medium_filter, rate, scale, carry),
        [table, table, cols(ROWS), cols(TAPS), cols(ROWS), cols(TAPS), dense, dense, dense],
        flops=2 * CHANS * POINTS * (POINTS + ROWS + TAPS),
    )
    mine = (ZH, 8, LANES)
    (spread,) = small(
        spread_sum_kernel, [shape((ZH,) + mine)], parts.reshape((Y * ZL,) + mine), token
    )
    parts = lax.all_to_all(spread, "zh", 0, 0, tiled=True)
    weighted, dots = large(
        weighted_kernel, [shape(FULL), shape(shares)], [cols(ROWS), whole(*shares)],
        (forward, inverse, grad_mixed, after, medium_filter, gate_key, stream, gain),
        [table, table, cols(ROWS), cols(TAPS), cols(TAPS), cols(ROWS), cols(ROWS), dense],
        scratch=[pltpu.VMEM((ROWS, LANES), F32)],
        flops=2 * CHANS * POINTS * (POINTS + ROWS + TAPS),
    )
    (spread,) = small(spread_sum_kernel, [shape((Y * ZL,) + mine)], parts, dots)
    dots = lax.all_to_all(dots, "chan", 0, 0, tiled=True)
    own_half = lax.all_to_all(spread, ("y", "zl"), 0, 0, tiled=True).reshape(PLANE, 8, LANES)
    grad_stream, token = large(
        stream_kernel, [shape(FULL, BF16), shape(DENSE)], [cols(ROWS), dense],
        (inv, dots, weighted, stream), [thin, whole(*shares)] + [cols(ROWS)] * 2,
        scratch=[pltpu.VMEM((ROWS, LANES), F32)],
    )
    (own_half,) = small(fence_kernel, [shape(own_half.shape)], own_half, token)
    other_half = lax.ppermute(own_half, "core", swap)
    grad_filter, grad_residue = small(
        finish_kernel, [shape((TAPS, CHANS)), shape(DENSE)], place, own_half, other_half, medium_filter,
        residue, specs=[SMEM] + [VMEM] * 4,
    )
    return (grad_query, grad_stream, grad_filter, grad_residue.reshape(CHANS))


def solution(mesh):
    devices = mesh.devices.reshape(Y, ZH, ZL, 2, mesh.devices.shape[1])
    fine = Mesh(devices, ("y", "zh", "zl", "core", "chan"))
    seq = ("y", "zh", "zl", "core")
    rows, chans = (P(seq, "chan"), P("chan"))
    in_specs = (rows, chans, rows, rows, rows, rows, P(None, "chan"), chans, chans)
    out_specs = (rows, rows, P(None, "chan"), chans)
    return jax.shard_map(body, mesh=fine, in_specs=in_specs, out_specs=out_specs, check_vma=False)
```

```python
import jax
import jax.numpy as jnp
import numpy as np
from jax import lax
from jax.experimental import pallas as pl
from jax.experimental.pallas import tpu as pltpu
from jax.sharding import Mesh, PartitionSpec as P

EPSILON = 1e-05
ROWS = 256
TAPS = 128
CHANS = 1024
TOKENS = 32768
CHANNEL_TOTAL = 4096
LANES = 128
TILES = CHANS // LANES
WIDTH = 256
PER = WIDTH // LANES
STEPS = CHANS // WIDTH
GROUPS = TAPS // 8
POINTS = ROWS + TAPS
HALF = POINTS // 2
X, Y, Z, ZL = (4, 4, 16, 4)
ZH = Z // ZL
PLANE = Y * Z
LARGE = 16 * 1024 * 1024
SMALL = 8 * 1024 * 1024
F32 = jnp.float32
BF16 = jnp.bfloat16
DENSE = (TILES, LANES)
FULL = (ROWS, CHANS)


def transform_tables():
    k = np.arange(HALF, dtype=np.int64)[:, None]
    n = np.arange(POINTS, dtype=np.int64)[None, :]
    angle = np.pi * (((2 * k + 1) * n) % (2 * POINTS)).astype(np.float64) / POINTS
    table = np.concatenate([np.cos(angle), -np.sin(angle)], axis=0)
    forward = table.astype(BF16)
    inverse = np.ascontiguousarray(table.T).astype(BF16)
    lags = np.ascontiguousarray(table.T[TAPS:0:-1]).astype(BF16)
    return forward, inverse, lags


ANY = pl.BlockSpec(memory_space=pl.ANY)
SMEM = pl.BlockSpec(memory_space=pltpu.SMEM)
VMEM = pl.BlockSpec(memory_space=pltpu.VMEM)


def shape(dims, dtype=F32):
    return jax.ShapeDtypeStruct(dims, dtype)


def cols(ref, step):
    return ref.at[:, pl.ds(step * WIDTH, WIDTH)]


def blocks(ref, step):
    return ref.at[:, pl.ds(step * PER, PER)]


def cost(args, outs, flops):
    sizes = [a.size * a.dtype.itemsize for a in args]
    sizes += [int(np.prod(o.shape)) * o.dtype.itemsize for o in outs]
    return pl.CostEstimate(flops=flops, bytes_accessed=sum(sizes), transcendentals=0)


def small(kernel, outs, *args, specs=None):
    return pl.pallas_call(
        kernel,
        out_shape=tuple(outs),
        in_specs=[VMEM] * len(args) if specs is None else specs,
        out_specs=tuple([VMEM] * len(outs)),
        compiler_params=pltpu.CompilerParams(vmem_limit_bytes=SMALL),
        cost_estimate=cost(args, outs, 0),
    )(*args)


def large(kernel, outs, out_cuts, args, in_cuts, scratch=(), flops=0):
    cuts = list(in_cuts) + list(out_cuts)
    cut_at = [i for i, cut in enumerate(cuts) if cut in (cols, blocks)]
    like = list(args) + list(outs)

    def stepped(*refs):
        count = len(cuts)
        far = list(refs[:count])
        extra = refs[count : count + len(scratch)]
        near = dict(zip(cut_at, refs[count + len(scratch) :]))
        sems = refs[-1]

        def copy(i, step):
            ends = [cuts[i](ref, step) for ref in (far[i], near[i])]
            if i >= len(args):
                ends.reverse()
            return pltpu.make_async_copy(*ends, sems.at[cut_at.index(i) * STEPS + step])

        loads = [[copy(i, step) for i in cut_at if i < len(args)] for step in range(STEPS)]
        stores = [[copy(i, step) for i in cut_at if i >= len(args)] for step in range(STEPS)]
        for step in range(STEPS):
            for load in loads[step]:
                load.start()
        for step in range(STEPS):
            for load in loads[step]:
                load.wait()
            views = [cuts[i](near[i], step) if i in near else far[i] for i in range(count)]
            kernel(step, *views, *extra)
            for store in stores[step]:
                store.start()
        for step in range(STEPS):
            for store in stores[step]:
                store.wait()

    specs = [ANY if i in cut_at else (VMEM if cuts[i] is None else cuts[i]) for i in range(len(cuts))]
    return pl.pallas_call(
        stepped,
        out_shape=tuple(outs),
        in_specs=specs[: len(args)],
        out_specs=tuple(specs[len(args) :]),
        scratch_shapes=list(scratch)
        + [pltpu.VMEM(like[i].shape, like[i].dtype) for i in cut_at]
        + [pltpu.SemaphoreType.DMA((len(cut_at) * STEPS,))],
        compiler_params=pltpu.CompilerParams(vmem_limit_bytes=LARGE),
        cost_estimate=pl.CostEstimate(flops=flops, bytes_accessed=1024, transcendentals=0),
    )(*args)


def dot(a, b):
    return lax.dot_general(
        a, b, (((1,), (0,)), ((), ())), preferred_element_type=F32
    )


def row(ref, step):
    at = step * PER
    return jnp.concatenate([ref[at + i : at + i + 1, :] for i in range(PER)], axis=1)


def put_row(ref, step, value):
    at = step * PER
    for i in range(PER):
        ref[at + i : at + i + 1, :] = value[:, i * LANES : (i + 1) * LANES]


def fold(value):
    return sum(value[:, i * LANES : (i + 1) * LANES] for i in range(PER))


def row_mean(total_ref):
    packed = total_ref[...] / CHANNEL_TOTAL
    return jnp.concatenate(
        [jnp.broadcast_to(packed[i : i + 1], (LANES, LANES)).T for i in range(ROWS // LANES)], axis=0
    )


def widen(value):
    return jnp.concatenate([value] * PER, axis=1)


def pack_rows(acc, out_ref):
    total = jnp.sum(acc.T, axis=0, keepdims=True)
    out_ref[...] = jnp.concatenate([total[:, :LANES], total[:, LANES:]], axis=0)


def squares_kernel(step, stream_ref, squares_ref, acc_ref):
    value = stream_ref[...].astype(F32)
    squares = fold(value * value)
    acc_ref[...] = squares if step == 0 else acc_ref[...] + squares
    if step == STEPS - 1:
        pack_rows(acc_ref[...], squares_ref)


def scan_kernel(step, out_ref, cot_ref, rate_ref, spread_ref, local_ref, first_ref):
    rank = lax.broadcasted_iota(jnp.int32, (8, WIDTH), 0)
    rate = row(rate_ref, step)
    source = out_ref[...].astype(F32) * cot_ref[...].astype(F32)
    coefs = [(s, jnp.where(rank < 8 - s, jnp.exp(-float(s) * rate), 0.0)) for s in (1, 2, 4)]
    power = jnp.exp(-rate * (8 - rank).astype(F32))
    carry = jnp.zeros((1, WIDTH), F32)
    for group in range(ROWS // 8 - 1, -1, -1):
        value = source[group * 8 : group * 8 + 8, :]
        for s, coef in coefs:
            value = value + coef * pltpu.roll(value, 8 - s, 0)
        value = value + power * carry
        local_ref[group * 8 : group * 8 + 8, :] = value
        carry = value[0:1, :]
    put_row(first_ref, step, carry)
    if step == STEPS - 1:
        spread_ref[...] = jnp.broadcast_to(first_ref[...], spread_ref.shape)


def column_kernel(place_ref, parts_ref, first_ref, rate_ref, out_ref):
    z = place_ref[1]
    pace = rate_ref[...] * (-2.0 * ROWS)
    ahead = jnp.zeros(DENSE, F32)
    total = jnp.zeros(DENSE, F32)
    for other in range(Z):
        value = parts_ref[other]
        gap = other - z - 1
        weight = jnp.exp(pace * jnp.maximum(gap, 0).astype(F32))
        ahead = ahead + jnp.where(gap >= 0, weight, 0.0) * value
        total = total + jnp.exp(pace * float(other)) * value
    count = out_ref.shape[0]
    out_ref[:, 0] = jnp.broadcast_to(total, (count,) + DENSE)
    out_ref[:, 1] = jnp.broadcast_to(ahead, (count,) + DENSE)
    out_ref[:, 2] = jnp.broadcast_to(first_ref[0], (count,) + DENSE)


def carry_kernel(place_ref, parts_ref, rate_ref, carry_ref):
    y, z, core = (place_ref[0], place_ref[1], place_ref[2])
    rate = rate_ref[...]
    decay = jnp.exp(-ROWS * rate)
    rest = jnp.exp(rate * (-2.0 * ROWS) * (Z - 1 - z).astype(F32))
    both = []
    for parity in range(2):
        planes = jnp.zeros(DENSE, F32)
        for later in range(1, Y):
            gap = later - y - 1
            weight = jnp.exp(rate * (-2.0 * ROWS * Z) * jnp.maximum(gap, 0).astype(F32))
            planes = planes + jnp.where(gap >= 0, weight, 0.0) * parts_ref[later * 2 + parity, 0]
        both.append(parts_ref[y * 2 + parity, 1] + rest * planes)
    last = both[0] + decay * both[1]
    carry_ref[...] = jnp.where(core == 0, parts_ref[y * 2 + 1, 2] + decay * last, last)


def product_kernel(step, total_ref, stream_ref, key_ref, gain_ref, product_ref, rim_ref, inv_ref):
    if step == 0:
        inv_ref[...] = lax.rsqrt(row_mean(total_ref) + EPSILON)

    normed = stream_ref[...].astype(F32) * widen(inv_ref[...]) * row(gain_ref, step)
    product = key_ref[...].astype(F32) * normed
    product_ref[...] = product.astype(BF16)
    rim_ref[...] = product[ROWS - TAPS :, :]


def mul_conj(a, b):
    ar, ai = (a[:HALF], a[HALF:])
    br, bi = (b[:HALF], b[HALF:])
    return jnp.concatenate([ar * br + ai * bi, ar * bi - ai * br], axis=0).astype(BF16)


def mul(a, b):
    ar, ai = (a[:HALF], a[HALF:])
    br, bi = (b[:HALF], b[HALF:])
    return jnp.concatenate([ar * br - ai * bi, ar * bi + ai * br], axis=0).astype(BF16)


def grad_stored(step, local_ref, rate_ref, scale_ref, carry_ref):
    rate = row(rate_ref, step)
    rank = lax.broadcasted_iota(jnp.int32, (8, WIDTH), 0)
    power = jnp.exp(-rate * (8 - rank).astype(F32)) * row(carry_ref, step)
    groups = []
    for group in range(ROWS // 8):
        far = power * jnp.exp(-rate * float(ROWS - 8 - 8 * group))
        groups.append(local_ref[group * 8 : group * 8 + 8, :] + far)
    return jnp.concatenate(groups, axis=0) * row(scale_ref, step)


def filter_kernel(
    step, place_ref, fwd_ref, lag_ref, product_ref, rim_ref, local_ref, query_ref, rate_ref, scale_ref, carry_ref,
    keep_ref, send_ref, mixed_grad_ref, head_ref,
):
    ext = jnp.concatenate([rim_ref[...].astype(BF16), product_ref[...]], axis=0)
    product = dot(fwd_ref[...], ext)
    grad_mixed = query_ref[...].astype(F32) * grad_stored(step, local_ref, rate_ref, scale_ref, carry_ref)
    head_ref[...] = grad_mixed[:TAPS]
    grad_mixed = grad_mixed.astype(BF16)
    mixed_grad_ref[...] = grad_mixed
    spectrum = dot(fwd_ref[:, :ROWS], grad_mixed)
    taps = dot(lag_ref[...], mul_conj(spectrum, product))
    is_first = place_ref[2] == 0
    for group in range(GROUPS // 2):
        low = taps[group * 8 : group * 8 + 8, :]
        high = taps[TAPS // 2 + group * 8 : TAPS // 2 + group * 8 + 8, :]
        keep = jnp.where(is_first, low, high)
        send = jnp.where(is_first, high, low)
        for i in range(PER):
            keep_ref[group, i] = keep[:, i * LANES : (i + 1) * LANES]
            send_ref[group, i] = send[:, i * LANES : (i + 1) * LANES]


def query_kernel(
    step, fwd_ref, inv_ref, product_ref, rim_ref, local_ref, filter_ref, rate_ref, scale_ref, carry_ref, grad_ref, token_ref
):
    ext = jnp.concatenate([rim_ref[...].astype(BF16), product_ref[...]], axis=0)
    product = dot(fwd_ref[...], ext)
    taps = dot(fwd_ref[:, :TAPS], filter_ref[...].astype(BF16))
    mixed = dot(inv_ref[TAPS:, :], mul(product, taps)) * (2.0 / POINTS)
    grad_ref[...] = (mixed * grad_stored(step, local_ref, rate_ref, scale_ref, carry_ref)).astype(BF16)
    if step == STEPS - 1:
        token_ref[...] = carry_ref[...]


def weighted_kernel(
    step, later_ref, fwd_ref, inv_ref, grad_ref, after_ref, filter_ref, key_ref, stream_ref, gain_ref, weighted_ref, dots_ref, acc_ref
):
    ext = jnp.concatenate([grad_ref[...], after_ref[...].astype(BF16)], axis=0)
    grad = dot(fwd_ref[...], ext)
    taps = dot(fwd_ref[:, :TAPS], filter_ref[...].astype(BF16))
    back = dot(inv_ref[:ROWS, :], mul_conj(taps, grad)) * (2.0 / POINTS)
    weighted = row(gain_ref, step) * key_ref[...].astype(F32) * back
    weighted_ref[...] = weighted
    dots = fold(weighted * stream_ref[...].astype(F32))

    if step == 0:
        acc_ref[...] = dots
    else:
        acc_ref[...] += dots

    if step == STEPS - 1:
        pack_rows(acc_ref[...], dots_ref)


def stream_kernel(step, inv_ref, dots_ref, weighted_ref, stream_ref, out_ref, factor_ref):
    inv = inv_ref[...]

    if step == 0:
        factor_ref[...] = inv * inv * row_mean(dots_ref)

    value = weighted_ref[...] - stream_ref[...].astype(F32) * widen(factor_ref[...])
    out_ref[...] = (widen(inv) * value).astype(BF16)


def fence_kernel(value_ref, after_ref, out_ref):
    pass


def after_all(value, *others):
    return pl.pallas_call(
        fence_kernel,
        out_shape=shape(value.shape, value.dtype),
        in_specs=[ANY] * (1 + len(others)),
        out_specs=ANY,
        input_output_aliases={0: 0},
        compiler_params=pltpu.CompilerParams(vmem_limit_bytes=LARGE),
    )(value, *others)


def gate_kernel(value_ref, after_ref, out_ref):
    out_ref[...] = value_ref[...]


def add_kernel(a_ref, b_ref, out_ref):
    out_ref[...] = a_ref[...] + b_ref[...]


def spread_sum_kernel(parts_ref, *refs):
    spread_ref = refs[-1]
    total = jnp.sum(parts_ref[...], axis=0)
    spread_ref[...] = jnp.broadcast_to(total, spread_ref.shape)


def finish_kernel(place_ref, own_ref, other_ref, filter_ref, residue_ref, filter_out, residue_out):
    scale = TOKENS ** (-0.5) * 2.0 / POINTS
    count = own_ref.shape[0]
    is_first = place_ref[2] == 0
    for tile in range(TILES):
        lanes = slice(tile * LANES, (tile + 1) * LANES)
        total = jnp.zeros((8, LANES), F32)
        for group in range(GROUPS):
            at = (group * TILES + tile) % count
            low = group * TILES + tile < count
            own, other = (own_ref[at], other_ref[at])
            value = jnp.where(is_first, own, other) if low else jnp.where(is_first, other, own)
            value = value * scale
            rows = slice(group * 8, group * 8 + 8)
            filter_out[rows, lanes] = value
            total = total + filter_ref[rows, lanes] * value
        total = jnp.sum(total, axis=0, keepdims=True)
        residue_out[tile : tile + 1, :] = total / residue_ref[tile : tile + 1, :]


def body(
    stream, norm_gain, gate_query, gate_key, gate_out, cotangent, medium_filter, long_residue, long_rate
):
    forward, inverse, lags = (jnp.asarray(t) for t in transform_tables())
    gain, rate, residue = (v.reshape(DENSE) for v in (norm_gain, long_rate, long_residue))
    scale = residue * jnp.sqrt(-jnp.expm1(-2.0 * rate))
    z_at = lax.axis_index(("zh", "zl"))
    place = jnp.stack([lax.axis_index("y"), z_at, lax.axis_index("core")]).astype(jnp.int32)
    swap = [(0, 1), (1, 0)]
    seq = ("y", "zh", "zl", "core")
    count = 2 * PLANE

    packed = (ROWS // LANES, LANES)
    spread, local = large(
        scan_kernel, [shape((Z,) + DENSE), shape(FULL)], [None, cols], (gate_out, cotangent, rate),
        [cols, cols, None], scratch=[pltpu.VMEM(DENSE, F32)],
    )
    column = lax.all_to_all(spread, ("zh", "zl"), 0, 0, tiled=True)
    (squares,) = large(
        squares_kernel, [shape(packed)], [None], (stream,), [cols], scratch=[pltpu.VMEM((ROWS, LANES), F32)]
    )
    squares = lax.psum(squares, "chan")
    product, rim, inv = large(
        product_kernel, [shape(FULL, BF16), shape((TAPS, CHANS)), shape((ROWS, LANES))],
        [cols, cols, None],
        (squares, stream, gate_key, gain), [None, cols, cols, None],
    )
    before = lax.ppermute(after_all(rim, column), seq, [(i, i + 1) for i in range(count - 1)])
    (sums,) = small(
        column_kernel, [shape((2 * Y, 3) + DENSE)], place, column, spread, rate, specs=[SMEM] + [VMEM] * 3
    )
    sums = lax.all_to_all(sums, ("y", "core"), 0, 0, tiled=True)
    (carry,) = small(carry_kernel, [shape(DENSE)], place, sums, rate, specs=[SMEM] + [VMEM] * 2)

    half = (GROUPS // 2, TILES, 8, LANES)
    keep, send, grad_mixed, head = large(
        filter_kernel, [shape(half), shape(half), shape(FULL, BF16), shape((TAPS, CHANS))],
        [blocks, blocks, cols, cols],
        (place, forward, lags, product, before, local, gate_query, rate, scale, carry),
        [SMEM, None, None, cols, cols, cols, cols, None, None, None],
        flops=2 * CHANS * POINTS * (POINTS + ROWS + TAPS),
    )

    got = lax.ppermute(send, "core", swap)
    (chip_sum,) = small(add_kernel, [shape(half)], keep, got)
    after = lax.ppermute(head, seq, [(i + 1, i) for i in range(count - 1)])
    parts = lax.all_to_all(chip_sum.reshape(PLANE, 8, LANES), ("y", "zl"), 0, 0, tiled=True)
    grad_query, token = large(
        query_kernel, [shape(FULL, BF16), shape(DENSE)], [cols, None],
        (forward, inverse, product, before, local, medium_filter, rate, scale, carry),
        [None, None, cols, cols, cols, cols, None, None, None],
        flops=2 * CHANS * POINTS * (POINTS + ROWS + TAPS),
    )
    mine = (ZH, 8, LANES)
    (spread,) = small(
        spread_sum_kernel, [shape((ZH,) + mine)], parts.reshape((Y * ZL,) + mine), token, specs=[VMEM, ANY]
    )
    parts = lax.all_to_all(spread, "zh", 0, 0, tiled=True)
    weighted, dots = large(
        weighted_kernel, [shape(FULL), shape(packed)], [cols, None],
        (spread, forward, inverse, grad_mixed, after, medium_filter, gate_key, stream, gain),
        [ANY, None, None, cols, cols, cols, cols, cols, None],
        scratch=[pltpu.VMEM((ROWS, LANES), F32)],
        flops=2 * CHANS * POINTS * (POINTS + ROWS + TAPS),
    )
    (spread,) = small(
        spread_sum_kernel, [shape((Y * ZL,) + mine)], parts, dots, specs=[VMEM, ANY]
    )
    dots = lax.psum(dots, "chan")
    own_half = lax.all_to_all(spread, ("y", "zl"), 0, 0, tiled=True).reshape(PLANE, 8, LANES)
    (grad_stream,) = large(
        stream_kernel, [shape(FULL, BF16)], [cols],
        (inv, dots, weighted, stream), [None, None] + [cols] * 2,
        scratch=[pltpu.VMEM((ROWS, LANES), F32)],
    )
    (own_half,) = small(gate_kernel, [shape(own_half.shape)], own_half, dots, specs=[VMEM, ANY])
    other_half = lax.ppermute(own_half, "core", swap)
    grad_filter, grad_residue = small(
        finish_kernel, [shape((TAPS, CHANS)), shape(DENSE)], place, own_half, other_half, medium_filter,
        residue, specs=[SMEM] + [VMEM] * 4,
    )
    return (grad_query, grad_stream, grad_filter, grad_residue.reshape(CHANS))


def solution(mesh):
    devices = mesh.devices.reshape(Y, ZH, ZL, 2, mesh.devices.shape[1])
    fine = Mesh(devices, ("y", "zh", "zl", "core", "chan"))
    seq = ("y", "zh", "zl", "core")
    rows, chans = (P(seq, "chan"), P("chan"))
    in_specs = (rows, chans, rows, rows, rows, rows, P(None, "chan"), chans, chans)
    out_specs = (rows, rows, P(None, "chan"), chans)
    return jax.shard_map(body, mesh=fine, in_specs=in_specs, out_specs=out_specs, check_vma=False)
```

```python
import jax
import jax.numpy as jnp
import numpy as np
from jax import lax
from jax.experimental import pallas as pl
from jax.experimental.pallas import tpu as pltpu
from jax.sharding import Mesh, PartitionSpec as P

EPSILON = 1e-05
ROWS = 256
TAPS = 128
CHANS = 1024
TOKENS = 32768
CHANNEL_TOTAL = 4096
LANES = 128
TILES = CHANS // LANES
WIDTH = 256
PER = WIDTH // LANES
STEPS = CHANS // WIDTH
GROUPS = TAPS // 8
POINTS = ROWS + TAPS
HALF = POINTS // 2
X, Y, Z, ZL = (4, 4, 16, 4)
ZH = Z // ZL
PLANE = Y * Z
LARGE = 16 * 1024 * 1024
SMALL = 8 * 1024 * 1024
F32 = jnp.float32
BF16 = jnp.bfloat16
DENSE = (TILES, LANES)
FULL = (ROWS, CHANS)


def transform_tables():
    k = np.arange(HALF, dtype=np.int64)[:, None]
    n = np.arange(POINTS, dtype=np.int64)[None, :]
    angle = np.pi * (((2 * k + 1) * n) % (2 * POINTS)).astype(np.float64) / POINTS
    table = np.concatenate([np.cos(angle), -np.sin(angle)], axis=0)
    forward = table.astype(BF16)
    inverse = np.ascontiguousarray(table.T).astype(BF16)
    lags = np.ascontiguousarray(table.T[TAPS:0:-1]).astype(BF16)
    return forward, inverse, lags


ANY = pl.BlockSpec(memory_space=pl.ANY)
VMEM = pl.BlockSpec(memory_space=pltpu.VMEM)


def shape(dims, dtype=F32):
    return jax.ShapeDtypeStruct(dims, dtype)


def cols(ref, step):
    return ref.at[:, pl.ds(step * WIDTH, WIDTH)]


def blocks(ref, step):
    return ref.at[:, pl.ds(step * PER, PER)]


def cost(args, outs, flops):
    sizes = [a.size * a.dtype.itemsize for a in args]
    sizes += [int(np.prod(o.shape)) * o.dtype.itemsize for o in outs]
    return pl.CostEstimate(flops=flops, bytes_accessed=sum(sizes), transcendentals=0)


def small(kernel, outs, *args, specs=None):
    return pl.pallas_call(
        kernel,
        out_shape=tuple(outs),
        in_specs=[VMEM] * len(args) if specs is None else specs,
        out_specs=tuple([VMEM] * len(outs)),
        compiler_params=pltpu.CompilerParams(vmem_limit_bytes=SMALL),
        cost_estimate=cost(args, outs, 0),
    )(*args)


def large(kernel, outs, out_cuts, args, in_cuts, scratch=(), flops=0, grant=LARGE):
    cuts = list(in_cuts) + list(out_cuts)

    def stepped(*refs):
        arrays, extra = (refs[: len(cuts)], refs[len(cuts) :])
        for step in range(STEPS):
            views = [cut(ref, step) if cut in (cols, blocks) else ref for cut, ref in zip(cuts, arrays)]
            kernel(step, *views, *extra)

    specs = [VMEM if cut in (cols, blocks, None) else cut for cut in cuts]
    return pl.pallas_call(
        stepped,
        out_shape=tuple(outs),
        in_specs=specs[: len(args)],
        out_specs=tuple(specs[len(args) :]),
        scratch_shapes=list(scratch),
        compiler_params=pltpu.CompilerParams(vmem_limit_bytes=grant),
        cost_estimate=pl.CostEstimate(flops=flops, bytes_accessed=1024, transcendentals=0),
    )(*args)


def dot(a, b):
    return lax.dot_general(
        a, b, (((1,), (0,)), ((), ())), preferred_element_type=F32
    )


def row(ref, step):
    at = step * PER
    return jnp.concatenate([ref[at + i : at + i + 1, :] for i in range(PER)], axis=1)


def put_row(ref, step, value):
    at = step * PER
    for i in range(PER):
        ref[at + i : at + i + 1, :] = value[:, i * LANES : (i + 1) * LANES]


def fold(value):
    return sum(value[:, i * LANES : (i + 1) * LANES] for i in range(PER))


def row_mean(total_ref):
    packed = total_ref[...] / CHANNEL_TOTAL
    return jnp.concatenate(
        [jnp.broadcast_to(packed[i : i + 1], (LANES, LANES)).T for i in range(ROWS // LANES)], axis=0
    )


def widen(value):
    return jnp.concatenate([value] * PER, axis=1)


def pack_rows(acc, out_ref):
    total = jnp.sum(acc.T, axis=0, keepdims=True)
    out_ref[...] = jnp.concatenate([total[:, :LANES], total[:, LANES:]], axis=0)


def squares_kernel(step, stream_ref, squares_ref, acc_ref):
    value = stream_ref[...].astype(F32)
    squares = fold(value * value)
    acc_ref[...] = squares if step == 0 else acc_ref[...] + squares
    if step == STEPS - 1:
        pack_rows(acc_ref[...], squares_ref)


def scan_kernel(step, out_ref, cot_ref, rate_ref, spread_ref, local_ref, first_ref):
    rank = lax.broadcasted_iota(jnp.int32, (8, WIDTH), 0)
    rate = row(rate_ref, step)
    source = out_ref[...].astype(F32) * cot_ref[...].astype(F32)
    coefs = [(s, jnp.where(rank < 8 - s, jnp.exp(-float(s) * rate), 0.0)) for s in (1, 2, 4)]
    power = jnp.exp(-rate * (8 - rank).astype(F32))
    carry = jnp.zeros((1, WIDTH), F32)
    for group in range(ROWS // 8 - 1, -1, -1):
        value = source[group * 8 : group * 8 + 8, :]
        for s, coef in coefs:
            value = value + coef * pltpu.roll(value, 8 - s, 0)
        value = value + power * carry
        local_ref[group * 8 : group * 8 + 8, :] = value
        carry = value[0:1, :]
    put_row(first_ref, step, carry)
    if step == STEPS - 1:
        spread_ref[...] = jnp.broadcast_to(first_ref[...], spread_ref.shape)


def column_kernel(parts_ref, first_ref, rate_ref, after_ref, out_ref):
    z = lax.axis_index(("zh", "zl"))
    pace = rate_ref[...] * (-2.0 * ROWS)
    ahead = jnp.zeros(DENSE, F32)
    total = jnp.zeros(DENSE, F32)
    for other in range(Z):
        value = parts_ref[other]
        gap = other - z - 1
        weight = jnp.exp(pace * jnp.maximum(gap, 0).astype(F32))
        ahead = ahead + jnp.where(gap >= 0, weight, 0.0) * value
        total = total + jnp.exp(pace * float(other)) * value
    count = out_ref.shape[0]
    out_ref[:, 0] = jnp.broadcast_to(total, (count,) + DENSE)
    out_ref[:, 1] = jnp.broadcast_to(ahead, (count,) + DENSE)
    out_ref[:, 2] = jnp.broadcast_to(first_ref[0], (count,) + DENSE)


def carry_kernel(parts_ref, rate_ref, carry_ref):
    y, z, core = (lax.axis_index("y"), lax.axis_index(("zh", "zl")), lax.axis_index("core"))
    rate = rate_ref[...]
    decay = jnp.exp(-ROWS * rate)
    rest = jnp.exp(rate * (-2.0 * ROWS) * (Z - 1 - z).astype(F32))
    both = []
    for parity in range(2):
        planes = jnp.zeros(DENSE, F32)
        for later in range(1, Y):
            gap = later - y - 1
            weight = jnp.exp(rate * (-2.0 * ROWS * Z) * jnp.maximum(gap, 0).astype(F32))
            planes = planes + jnp.where(gap >= 0, weight, 0.0) * parts_ref[later * 2 + parity, 0]
        both.append(parts_ref[y * 2 + parity, 1] + rest * planes)
    last = both[0] + decay * both[1]
    carry_ref[...] = jnp.where(core == 0, parts_ref[y * 2 + 1, 2] + decay * last, last)


def product_kernel(step, after_ref, total_ref, stream_ref, key_ref, gain_ref, product_ref, rim_ref, inv_ref):
    if step == 0:
        inv_ref[...] = lax.rsqrt(row_mean(total_ref) + EPSILON)

    normed = stream_ref[...].astype(F32) * widen(inv_ref[...]) * row(gain_ref, step)
    product = key_ref[...].astype(F32) * normed
    product_ref[...] = product.astype(BF16)
    rim_ref[...] = product[ROWS - TAPS :, :]


def mul_conj(a, b):
    ar, ai = (a[:HALF], a[HALF:])
    br, bi = (b[:HALF], b[HALF:])
    return jnp.concatenate([ar * br + ai * bi, ar * bi - ai * br], axis=0).astype(BF16)


def mul(a, b):
    ar, ai = (a[:HALF], a[HALF:])
    br, bi = (b[:HALF], b[HALF:])
    return jnp.concatenate([ar * br - ai * bi, ar * bi + ai * br], axis=0).astype(BF16)


def grad_stored(step, local_ref, rate_ref, scale_ref, carry_ref):
    rate = row(rate_ref, step)
    rank = lax.broadcasted_iota(jnp.int32, (8, WIDTH), 0)
    power = jnp.exp(-rate * (8 - rank).astype(F32)) * row(carry_ref, step)
    groups = []
    for group in range(ROWS // 8):
        far = power * jnp.exp(-rate * float(ROWS - 8 - 8 * group))
        groups.append(local_ref[group * 8 : group * 8 + 8, :] + far)
    return jnp.concatenate(groups, axis=0) * row(scale_ref, step)


def filter_kernel(
    step, fwd_ref, lag_ref, product_ref, rim_ref, local_ref, query_ref, rate_ref, scale_ref, carry_ref,
    keep_ref, send_ref, mixed_grad_ref, head_ref,
):
    ext = jnp.concatenate([rim_ref[...].astype(BF16), product_ref[...]], axis=0)
    product = dot(fwd_ref[...], ext)
    grad_mixed = query_ref[...].astype(F32) * grad_stored(step, local_ref, rate_ref, scale_ref, carry_ref)
    head_ref[...] = grad_mixed[:TAPS]
    grad_mixed = grad_mixed.astype(BF16)
    mixed_grad_ref[...] = grad_mixed
    spectrum = dot(fwd_ref[:, :ROWS], grad_mixed)
    taps = dot(lag_ref[...], mul_conj(spectrum, product))
    is_first = lax.axis_index("core") == 0
    for group in range(GROUPS // 2):
        low = taps[group * 8 : group * 8 + 8, :]
        high = taps[TAPS // 2 + group * 8 : TAPS // 2 + group * 8 + 8, :]
        keep = jnp.where(is_first, low, high)
        send = jnp.where(is_first, high, low)
        for i in range(PER):
            keep_ref[group, i] = keep[:, i * LANES : (i + 1) * LANES]
            send_ref[group, i] = send[:, i * LANES : (i + 1) * LANES]


def query_kernel(
    step, fwd_ref, inv_ref, product_ref, rim_ref, local_ref, filter_ref, rate_ref, scale_ref, carry_ref, grad_ref, token_ref
):
    ext = jnp.concatenate([rim_ref[...].astype(BF16), product_ref[...]], axis=0)
    product = dot(fwd_ref[...], ext)
    taps = dot(fwd_ref[:, :TAPS], filter_ref[...].astype(BF16))
    mixed = dot(inv_ref[TAPS:, :], mul(product, taps)) * (2.0 / POINTS)
    grad_ref[...] = (mixed * grad_stored(step, local_ref, rate_ref, scale_ref, carry_ref)).astype(BF16)
    if step == STEPS - 1:
        token_ref[...] = carry_ref[...]


def weighted_kernel(
    step, later_ref, fwd_ref, inv_ref, grad_ref, after_ref, filter_ref, key_ref, stream_ref, gain_ref, weighted_ref, dots_ref, acc_ref
):
    ext = jnp.concatenate([grad_ref[...], after_ref[...].astype(BF16)], axis=0)
    grad = dot(fwd_ref[...], ext)
    taps = dot(fwd_ref[:, :TAPS], filter_ref[...].astype(BF16))
    back = dot(inv_ref[:ROWS, :], mul_conj(taps, grad)) * (2.0 / POINTS)
    weighted = row(gain_ref, step) * key_ref[...].astype(F32) * back
    weighted_ref[...] = weighted
    dots = fold(weighted * stream_ref[...].astype(F32))

    if step == 0:
        acc_ref[...] = dots
    else:
        acc_ref[...] += dots

    if step == STEPS - 1:
        pack_rows(acc_ref[...], dots_ref)


def stream_kernel(step, total_ref, dots_ref, weighted_ref, stream_ref, out_ref, inv_ref, factor_ref):
    if step == 0:
        inv_ref[...] = lax.rsqrt(row_mean(total_ref) + EPSILON)
        factor_ref[...] = inv_ref[...] * inv_ref[...] * row_mean(dots_ref)

    value = weighted_ref[...] - stream_ref[...].astype(F32) * widen(factor_ref[...])
    out_ref[...] = (widen(inv_ref[...]) * value).astype(BF16)


def gate_kernel(value_ref, after_ref, out_ref):
    out_ref[...] = value_ref[...]


def add_kernel(a_ref, b_ref, out_ref):
    out_ref[...] = a_ref[...] + b_ref[...]


def spread_sum_kernel(parts_ref, *refs):
    spread_ref = refs[-1]
    total = jnp.sum(parts_ref[...], axis=0)
    spread_ref[...] = jnp.broadcast_to(total, spread_ref.shape)


def finish_kernel(own_ref, other_ref, filter_ref, residue_ref, filter_out, residue_out):
    scale = TOKENS ** (-0.5) * 2.0 / POINTS
    count = own_ref.shape[0]
    is_first = lax.axis_index("core") == 0
    for tile in range(TILES):
        lanes = slice(tile * LANES, (tile + 1) * LANES)
        total = jnp.zeros((8, LANES), F32)
        for group in range(GROUPS):
            at = (group * TILES + tile) % count
            low = group * TILES + tile < count
            own, other = (own_ref[at], other_ref[at])
            value = jnp.where(is_first, own, other) if low else jnp.where(is_first, other, own)
            value = value * scale
            rows = slice(group * 8, group * 8 + 8)
            filter_out[rows, lanes] = value
            total = total + filter_ref[rows, lanes] * value
        total = jnp.sum(total, axis=0, keepdims=True)
        residue_out[tile : tile + 1, :] = total / residue_ref[tile : tile + 1, :]


def body(
    stream, norm_gain, gate_query, gate_key, gate_out, cotangent, medium_filter, long_residue, long_rate
):
    forward, inverse, lags = (jnp.asarray(t) for t in transform_tables())
    gain, rate, residue = (v.reshape(DENSE) for v in (norm_gain, long_rate, long_residue))
    scale = residue * jnp.sqrt(-jnp.expm1(-2.0 * rate))
    swap = [(0, 1), (1, 0)]
    seq = ("y", "zh", "zl", "core")
    count = 2 * PLANE

    packed = (ROWS // LANES, LANES)
    spread, local = large(
        scan_kernel, [shape((Z,) + DENSE), shape(FULL)], [None, cols], (gate_out, cotangent, rate),
        [cols, cols, None], scratch=[pltpu.VMEM(DENSE, F32)], grant=60 * 1024 * 1024,
    )
    column = lax.all_to_all(spread, ("zh", "zl"), 0, 0, tiled=True)
    (squares,) = large(
        squares_kernel, [shape(packed)], [None], (stream,), [cols], scratch=[pltpu.VMEM((ROWS, LANES), F32)]
    )
    squares = lax.psum(squares, "chan")
    product, rim = large(
        product_kernel, [shape(FULL, BF16), shape((TAPS, CHANS))], [cols, cols],
        (column, squares, stream, gate_key, gain), [ANY, None, cols, cols, None],
        scratch=[pltpu.VMEM((ROWS, LANES), F32)],
    )
    before = lax.ppermute(rim, seq, [(i, i + 1) for i in range(count - 1)])
    (sums,) = small(
        column_kernel, [shape((2 * Y, 3) + DENSE)], column, spread, rate, scale
    )
    sums = lax.all_to_all(sums, ("y", "core"), 0, 0, tiled=True)
    (carry,) = small(carry_kernel, [shape(DENSE)], sums, rate)

    half = (GROUPS // 2, TILES, 8, LANES)
    keep, send, grad_mixed, head = large(
        filter_kernel, [shape(half), shape(half), shape(FULL, BF16), shape((TAPS, CHANS))],
        [blocks, blocks, cols, cols],
        (forward, lags, product, before, local, gate_query, rate, scale, carry),
        [None, None, cols, cols, cols, cols, None, None, None],
        flops=2 * CHANS * POINTS * (POINTS + ROWS + TAPS),
    )

    got = lax.ppermute(send, "core", swap)
    (chip_sum,) = small(add_kernel, [shape(half)], keep, got)
    after = lax.ppermute(head, seq, [(i + 1, i) for i in range(count - 1)])
    parts = lax.all_to_all(chip_sum.reshape(PLANE, 8, LANES), ("y", "zl"), 0, 0, tiled=True)
    grad_query, token = large(
        query_kernel, [shape(FULL, BF16), shape(DENSE)], [cols, None],
        (forward, inverse, product, before, local, medium_filter, rate, scale, carry),
        [None, None, cols, cols, cols, cols, None, None, None],
        flops=2 * CHANS * POINTS * (POINTS + ROWS + TAPS),
    )
    mine = (ZH, 8, LANES)
    (spread,) = small(
        spread_sum_kernel, [shape((ZH,) + mine)], parts.reshape((Y * ZL,) + mine), token, specs=[VMEM, ANY]
    )
    parts = lax.all_to_all(spread, "zh", 0, 0, tiled=True)
    weighted, dots = large(
        weighted_kernel, [shape(FULL), shape(packed)], [cols, None],
        (spread, forward, inverse, grad_mixed, after, medium_filter, gate_key, stream, gain),
        [ANY, None, None, cols, cols, cols, cols, cols, None],
        scratch=[pltpu.VMEM((ROWS, LANES), F32)],
        flops=2 * CHANS * POINTS * (POINTS + ROWS + TAPS),
    )
    (spread,) = small(
        spread_sum_kernel, [shape((Y * ZL,) + mine)], parts, dots, specs=[VMEM, ANY]
    )
    dots = lax.psum(dots, "chan")
    own_half = lax.all_to_all(spread, ("y", "zl"), 0, 0, tiled=True).reshape(PLANE, 8, LANES)
    (grad_stream,) = large(
        stream_kernel, [shape(FULL, BF16)], [cols],
        (squares, dots, weighted, stream), [None, None] + [cols] * 2,
        scratch=[pltpu.VMEM((ROWS, LANES), F32)] * 2,
    )
    (own_half,) = small(gate_kernel, [shape(own_half.shape)], own_half, dots, specs=[VMEM, ANY])
    other_half = lax.ppermute(own_half, "core", swap)
    grad_filter, grad_residue = small(
        finish_kernel, [shape((TAPS, CHANS)), shape(DENSE)], own_half, other_half, medium_filter,
        residue,
    )
    return (grad_query, grad_stream, grad_filter, grad_residue.reshape(CHANS))


def solution(mesh):
    devices = mesh.devices.reshape(Y, ZH, ZL, 2, mesh.devices.shape[1])
    fine = Mesh(devices, ("y", "zh", "zl", "core", "chan"))
    seq = ("y", "zh", "zl", "core")
    rows, chans = (P(seq, "chan"), P("chan"))
    in_specs = (rows, chans, rows, rows, rows, rows, P(None, "chan"), chans, chans)
    out_specs = (rows, rows, P(None, "chan"), chans)
    return jax.shard_map(body, mesh=fine, in_specs=in_specs, out_specs=out_specs, check_vma=False)
```

```python
import jax
import jax.numpy as jnp
import numpy as np
from jax import lax
from jax.experimental import pallas as pl
from jax.experimental.pallas import tpu as pltpu
from jax.sharding import Mesh, PartitionSpec as P

EPSILON = 1e-05
ROWS = 256
TAPS = 128
CHANS = 1024
TOKENS = 32768
CHANNEL_TOTAL = 4096
LANES = 128
TILES = CHANS // LANES
WIDTH = 256
PER = WIDTH // LANES
STEPS = CHANS // WIDTH
GROUPS = TAPS // 8
POINTS = ROWS + TAPS
HALF = POINTS // 2
X, Y, Z, ZL = (4, 4, 16, 4)
ZH = Z // ZL
PLANE = Y * Z
LARGE = 16 * 1024 * 1024
SMALL = 8 * 1024 * 1024
F32 = jnp.float32
BF16 = jnp.bfloat16
DENSE = (TILES, LANES)
FULL = (ROWS, CHANS)


def transform_table():
    k = np.arange(HALF, dtype=np.int64)[:, None]
    n = np.arange(POINTS, dtype=np.int64)[None, :]
    angle = np.pi * (((2 * k + 1) * n) % (2 * POINTS)).astype(np.float64) / POINTS
    table = np.concatenate([np.cos(angle), -np.sin(angle)], axis=0)
    return table.astype(BF16)


ANY = pl.BlockSpec(memory_space=pl.ANY)
VMEM = pl.BlockSpec(memory_space=pltpu.VMEM)


def shape(dims, dtype=F32):
    return jax.ShapeDtypeStruct(dims, dtype)


def cols(ref, step):
    return ref.at[:, pl.ds(step * WIDTH, WIDTH)]


def blocks(ref, step):
    return ref.at[:, pl.ds(step * PER, PER)]


def cost(args, outs, flops):
    sizes = [a.size * a.dtype.itemsize for a in args]
    sizes += [int(np.prod(o.shape)) * o.dtype.itemsize for o in outs]
    return pl.CostEstimate(flops=flops, bytes_accessed=sum(sizes), transcendentals=0)


def small(kernel, outs, *args, specs=None):
    return pl.pallas_call(
        kernel,
        out_shape=tuple(outs),
        in_specs=[VMEM] * len(args) if specs is None else specs,
        out_specs=tuple([VMEM] * len(outs)),
        compiler_params=pltpu.CompilerParams(vmem_limit_bytes=SMALL),
        cost_estimate=cost(args, outs, 0),
    )(*args)


def large(kernel, outs, out_cuts, args, in_cuts, scratch=(), flops=0, grant=LARGE):
    cuts = list(in_cuts) + list(out_cuts)

    def stepped(*refs):
        arrays, extra = (refs[: len(cuts)], refs[len(cuts) :])
        for step in range(STEPS):
            views = [cut(ref, step) if cut in (cols, blocks) else ref for cut, ref in zip(cuts, arrays)]
            kernel(step, *views, *extra)

    specs = [VMEM if cut in (cols, blocks, None) else cut for cut in cuts]
    return pl.pallas_call(
        stepped,
        out_shape=tuple(outs),
        in_specs=specs[: len(args)],
        out_specs=tuple(specs[len(args) :]),
        scratch_shapes=list(scratch),
        compiler_params=pltpu.CompilerParams(vmem_limit_bytes=grant),
        cost_estimate=pl.CostEstimate(flops=flops, bytes_accessed=1024, transcendentals=0),
    )(*args)


def dot(a, b):
    return lax.dot_general(
        a, b, (((1,), (0,)), ((), ())), preferred_element_type=F32
    )


def dot_back(table, b):
    return lax.dot_general(
        table, b, (((0,), (0,)), ((), ())), preferred_element_type=F32
    )


def row(ref, step):
    at = step * PER
    return jnp.concatenate([ref[at + i : at + i + 1, :] for i in range(PER)], axis=1)


def put_row(ref, step, value):
    at = step * PER
    for i in range(PER):
        ref[at + i : at + i + 1, :] = value[:, i * LANES : (i + 1) * LANES]


def fold(value):
    return sum(value[:, i * LANES : (i + 1) * LANES] for i in range(PER))


def row_mean(total_ref):
    packed = total_ref[...] / CHANNEL_TOTAL
    return jnp.concatenate(
        [jnp.broadcast_to(packed[i : i + 1], (LANES, LANES)).T for i in range(ROWS // LANES)], axis=0
    )


def widen(value):
    return jnp.concatenate([value] * PER, axis=1)


def pack_rows(acc, out_ref):
    total = jnp.sum(acc.T, axis=0, keepdims=True)
    out_ref[...] = jnp.concatenate([total[:, :LANES], total[:, LANES:]], axis=0)


def squares_kernel(step, stream_ref, squares_ref, acc_ref):
    value = stream_ref[...].astype(F32)
    squares = fold(value * value)
    acc_ref[...] = squares if step == 0 else acc_ref[...] + squares
    if step == STEPS - 1:
        pack_rows(acc_ref[...], squares_ref)


def scan_kernel(step, out_ref, cot_ref, rate_ref, spread_ref, local_ref, first_ref):
    rank = lax.broadcasted_iota(jnp.int32, (8, WIDTH), 0)
    rate = row(rate_ref, step)
    source = out_ref[...].astype(F32) * cot_ref[...].astype(F32)
    coefs = [(s, jnp.where(rank < 8 - s, jnp.exp(-float(s) * rate), 0.0)) for s in (1, 2, 4)]
    power = jnp.exp(-rate * (8 - rank).astype(F32))
    carry = jnp.zeros((1, WIDTH), F32)
    for group in range(ROWS // 8 - 1, -1, -1):
        value = source[group * 8 : group * 8 + 8, :]
        for s, coef in coefs:
            value = value + coef * pltpu.roll(value, 8 - s, 0)
        value = value + power * carry
        local_ref[group * 8 : group * 8 + 8, :] = value
        carry = value[0:1, :]
    put_row(first_ref, step, carry)
    if step == STEPS - 1:
        spread_ref[...] = jnp.broadcast_to(first_ref[...], spread_ref.shape)


def column_kernel(parts_ref, rate_ref, after_ref, out_ref):
    z = lax.axis_index(("zh", "zl"))
    pace = rate_ref[...] * (-2.0 * ROWS)
    ahead = jnp.zeros(DENSE, F32)
    total = jnp.zeros(DENSE, F32)
    for other in range(Z):
        value = parts_ref[other]
        gap = other - z - 1
        weight = jnp.exp(pace * jnp.maximum(gap, 0).astype(F32))
        ahead = ahead + jnp.where(gap >= 0, weight, 0.0) * value
        total = total + jnp.exp(pace * float(other)) * value
    count = out_ref.shape[0]
    out_ref[:, 0] = jnp.broadcast_to(total, (count,) + DENSE)
    out_ref[:, 1] = jnp.broadcast_to(ahead, (count,) + DENSE)
    out_ref[:, 2] = jnp.broadcast_to(parts_ref[z], (count,) + DENSE)


def carry_kernel(parts_ref, rate_ref, carry_ref):
    y, z, core = (lax.axis_index("y"), lax.axis_index(("zh", "zl")), lax.axis_index("core"))
    rate = rate_ref[...]
    decay = jnp.exp(-ROWS * rate)
    rest = jnp.exp(rate * (-2.0 * ROWS) * (Z - 1 - z).astype(F32))
    both = []
    for parity in range(2):
        planes = jnp.zeros(DENSE, F32)
        for later in range(1, Y):
            gap = later - y - 1
            weight = jnp.exp(rate * (-2.0 * ROWS * Z) * jnp.maximum(gap, 0).astype(F32))
            planes = planes + jnp.where(gap >= 0, weight, 0.0) * parts_ref[later * 2 + parity, 0]
        both.append(parts_ref[y * 2 + parity, 1] + rest * planes)
    last = both[0] + decay * both[1]
    carry_ref[...] = jnp.where(core == 0, parts_ref[y * 2 + 1, 2] + decay * last, last)


def product_kernel(step, after_ref, total_ref, stream_ref, key_ref, gain_ref, product_ref, rim_ref, inv_ref):
    if step == 0:
        inv_ref[...] = lax.rsqrt(row_mean(total_ref) + EPSILON)

    normed = stream_ref[...].astype(F32) * widen(inv_ref[...]) * row(gain_ref, step)
    product = key_ref[...].astype(F32) * normed
    product_ref[...] = product.astype(BF16)
    rim_ref[...] = product[ROWS - TAPS :, :]


def mul_conj(a, b):
    ar, ai = (a[:HALF], a[HALF:])
    br, bi = (b[:HALF], b[HALF:])
    return jnp.concatenate([ar * br + ai * bi, ar * bi - ai * br], axis=0).astype(BF16)


def mul(a, b):
    ar, ai = (a[:HALF], a[HALF:])
    br, bi = (b[:HALF], b[HALF:])
    return jnp.concatenate([ar * br - ai * bi, ar * bi + ai * br], axis=0).astype(BF16)


def grad_stored(step, local_ref, rate_ref, scale_ref, carry_ref):
    rate = row(rate_ref, step)
    rank = lax.broadcasted_iota(jnp.int32, (8, WIDTH), 0)
    power = jnp.exp(-rate * (8 - rank).astype(F32)) * row(carry_ref, step)
    groups = []
    for group in range(ROWS // 8):
        far = power * jnp.exp(-rate * float(ROWS - 8 - 8 * group))
        groups.append(local_ref[group * 8 : group * 8 + 8, :] + far)
    return jnp.concatenate(groups, axis=0) * row(scale_ref, step)


def filter_kernel(
    step, fwd_ref, product_ref, rim_ref, local_ref, query_ref, rate_ref, scale_ref, carry_ref,
    keep_ref, send_ref, mixed_grad_ref, head_ref,
):
    ext = jnp.concatenate([rim_ref[...].astype(BF16), product_ref[...]], axis=0)
    product = dot(fwd_ref[...], ext)
    grad_mixed = query_ref[...].astype(F32) * grad_stored(step, local_ref, rate_ref, scale_ref, carry_ref)
    head_ref[...] = grad_mixed[:TAPS]
    grad_mixed = grad_mixed.astype(BF16)
    mixed_grad_ref[...] = grad_mixed
    spectrum = dot(fwd_ref[:, :ROWS], grad_mixed)
    taps = -dot_back(fwd_ref[:, ROWS:], mul_conj(product, spectrum))
    is_first = lax.axis_index("core") == 0
    for group in range(GROUPS // 2):
        low = taps[group * 8 : group * 8 + 8, :]
        high = taps[TAPS // 2 + group * 8 : TAPS // 2 + group * 8 + 8, :]
        keep = jnp.where(is_first, low, high)
        send = jnp.where(is_first, high, low)
        for i in range(PER):
            keep_ref[group, i] = keep[:, i * LANES : (i + 1) * LANES]
            send_ref[group, i] = send[:, i * LANES : (i + 1) * LANES]


def query_kernel(
    step, fwd_ref, product_ref, rim_ref, local_ref, filter_ref, rate_ref, scale_ref, carry_ref, grad_ref, token_ref
):
    ext = jnp.concatenate([rim_ref[...].astype(BF16), product_ref[...]], axis=0)
    product = dot(fwd_ref[...], ext)
    taps = dot(fwd_ref[:, :TAPS], filter_ref[...].astype(BF16))
    mixed = dot_back(fwd_ref[:, TAPS:], mul(product, taps)) * (2.0 / POINTS)
    grad_ref[...] = (mixed * grad_stored(step, local_ref, rate_ref, scale_ref, carry_ref)).astype(BF16)
    if step == STEPS - 1:
        token_ref[...] = carry_ref[...]


def weighted_kernel(
    step, later_ref, fwd_ref, grad_ref, after_ref, filter_ref, key_ref, stream_ref, gain_ref, weighted_ref, dots_ref, acc_ref
):
    ext = jnp.concatenate([grad_ref[...], after_ref[...].astype(BF16)], axis=0)
    grad = dot(fwd_ref[...], ext)
    taps = dot(fwd_ref[:, :TAPS], filter_ref[...].astype(BF16))
    back = dot_back(fwd_ref[:, :ROWS], mul_conj(taps, grad)) * (2.0 / POINTS)
    weighted = row(gain_ref, step) * key_ref[...].astype(F32) * back
    weighted_ref[...] = weighted
    dots = fold(weighted * stream_ref[...].astype(F32))

    if step == 0:
        acc_ref[...] = dots
    else:
        acc_ref[...] += dots

    if step == STEPS - 1:
        pack_rows(acc_ref[...], dots_ref)


def stream_kernel(step, total_ref, dots_ref, weighted_ref, stream_ref, out_ref, inv_ref, factor_ref):
    if step == 0:
        inv_ref[...] = lax.rsqrt(row_mean(total_ref) + EPSILON)
        factor_ref[...] = inv_ref[...] * inv_ref[...] * row_mean(dots_ref)

    value = weighted_ref[...] - stream_ref[...].astype(F32) * widen(factor_ref[...])
    out_ref[...] = (widen(inv_ref[...]) * value).astype(BF16)


def gate_kernel(value_ref, after_ref, out_ref):
    out_ref[...] = value_ref[...]


def add_kernel(a_ref, b_ref, out_ref):
    out_ref[...] = a_ref[...] + b_ref[...]


def spread_sum_kernel(parts_ref, *refs):
    spread_ref = refs[-1]
    total = jnp.sum(parts_ref[...], axis=0)
    spread_ref[...] = jnp.broadcast_to(total, spread_ref.shape)


def finish_kernel(own_ref, other_ref, filter_ref, residue_ref, filter_out, residue_out):
    scale = TOKENS ** (-0.5) * 2.0 / POINTS
    count = own_ref.shape[0]
    is_first = lax.axis_index("core") == 0
    for tile in range(TILES):
        lanes = slice(tile * LANES, (tile + 1) * LANES)
        total = jnp.zeros((8, LANES), F32)
        for group in range(GROUPS):
            at = (group * TILES + tile) % count
            low = group * TILES + tile < count
            own, other = (own_ref[at], other_ref[at])
            value = jnp.where(is_first, own, other) if low else jnp.where(is_first, other, own)
            value = value * scale
            rows = slice(group * 8, group * 8 + 8)
            filter_out[rows, lanes] = value
            total = total + filter_ref[rows, lanes] * value
        total = jnp.sum(total, axis=0, keepdims=True)
        residue_out[tile : tile + 1, :] = total / residue_ref[tile : tile + 1, :]


def body(
    stream, norm_gain, gate_query, gate_key, gate_out, cotangent, medium_filter, long_residue, long_rate
):
    forward = jnp.asarray(transform_table())
    gain, rate, residue = (v.reshape(DENSE) for v in (norm_gain, long_rate, long_residue))
    scale = residue * jnp.sqrt(-jnp.expm1(-2.0 * rate))
    swap = [(0, 1), (1, 0)]
    seq = ("y", "zh", "zl", "core")
    count = 2 * PLANE

    packed = (ROWS // LANES, LANES)
    spread, local = large(
        scan_kernel, [shape((Z,) + DENSE), shape(FULL)], [None, cols], (gate_out, cotangent, rate),
        [cols, cols, None], scratch=[pltpu.VMEM(DENSE, F32)], grant=60 * 1024 * 1024,
    )
    column = lax.all_to_all(spread, ("zh", "zl"), 0, 0, tiled=True)
    (squares,) = large(
        squares_kernel, [shape(packed)], [None], (stream,), [cols], scratch=[pltpu.VMEM((ROWS, LANES), F32)]
    )
    squares = lax.psum(squares, "chan")
    product, rim = large(
        product_kernel, [shape(FULL, BF16), shape((TAPS, CHANS))], [cols, cols],
        (column, squares, stream, gate_key, gain), [None, None, cols, cols, None],
        scratch=[pltpu.VMEM((ROWS, LANES), F32)],
    )
    before = lax.ppermute(rim, seq, [(i, i + 1) for i in range(count - 1)])
    (sums,) = small(
        column_kernel, [shape((2 * Y, 3) + DENSE)], column, rate, scale
    )
    sums = lax.all_to_all(sums, ("y", "core"), 0, 0, tiled=True)
    (carry,) = small(carry_kernel, [shape(DENSE)], sums, rate)

    half = (GROUPS // 2, TILES, 8, LANES)
    keep, send, grad_mixed, head = large(
        filter_kernel, [shape(half), shape(half), shape(FULL, BF16), shape((TAPS, CHANS))],
        [blocks, blocks, cols, cols],
        (forward, product, before, local, gate_query, rate, scale, carry),
        [None, cols, cols, cols, cols, None, None, None],
        flops=2 * CHANS * POINTS * (POINTS + ROWS + TAPS),
    )

    got = lax.ppermute(send, "core", swap)
    (chip_sum,) = small(add_kernel, [shape(half)], keep, got)
    after = lax.ppermute(head, seq, [(i + 1, i) for i in range(count - 1)])
    parts = lax.all_to_all(chip_sum.reshape(PLANE, 8, LANES), ("y", "zl"), 0, 0, tiled=True)
    grad_query, token = large(
        query_kernel, [shape(FULL, BF16), shape(DENSE)], [cols, None],
        (forward, product, before, local, medium_filter, rate, scale, carry),
        [None, cols, cols, cols, cols, None, None, None],
        flops=2 * CHANS * POINTS * (POINTS + ROWS + TAPS),
    )
    mine = (ZH, 8, LANES)
    (spread,) = small(
        spread_sum_kernel, [shape((ZH,) + mine)], parts.reshape((Y * ZL,) + mine), token, specs=[VMEM, ANY]
    )
    parts = lax.all_to_all(spread, "zh", 0, 0, tiled=True)
    weighted, dots = large(
        weighted_kernel, [shape(FULL), shape(packed)], [cols, None],
        (spread, forward, grad_mixed, after, medium_filter, gate_key, stream, gain),
        [ANY, None, cols, cols, cols, cols, cols, None],
        scratch=[pltpu.VMEM((ROWS, LANES), F32)],
        flops=2 * CHANS * POINTS * (POINTS + ROWS + TAPS),
    )
    (spread,) = small(
        spread_sum_kernel, [shape((Y * ZL,) + mine)], parts, dots, specs=[VMEM, ANY]
    )
    dots = lax.psum(dots, "chan")
    own_half = lax.all_to_all(spread, ("y", "zl"), 0, 0, tiled=True).reshape(PLANE, 8, LANES)
    (grad_stream,) = large(
        stream_kernel, [shape(FULL, BF16)], [cols],
        (squares, dots, weighted, stream), [None, None] + [cols] * 2,
        scratch=[pltpu.VMEM((ROWS, LANES), F32)] * 2,
    )
    (own_half,) = small(gate_kernel, [shape(own_half.shape)], own_half, dots, specs=[VMEM, ANY])
    other_half = lax.ppermute(own_half, "core", swap)
    grad_filter, grad_residue = small(
        finish_kernel, [shape((TAPS, CHANS)), shape(DENSE)], own_half, other_half, medium_filter,
        residue,
    )
    return (grad_query, grad_stream, grad_filter, grad_residue.reshape(CHANS))


def solution(mesh):
    devices = mesh.devices.reshape(Y, ZH, ZL, 2, mesh.devices.shape[1])
    fine = Mesh(devices, ("y", "zh", "zl", "core", "chan"))
    seq = ("y", "zh", "zl", "core")
    rows, chans = (P(seq, "chan"), P("chan"))
    in_specs = (rows, chans, rows, rows, rows, rows, P(None, "chan"), chans, chans)
    out_specs = (rows, rows, P(None, "chan"), chans)
    return jax.shard_map(body, mesh=fine, in_specs=in_specs, out_specs=out_specs, check_vma=False)
```

```python
import jax
import jax.numpy as jnp
import numpy as np
from jax import lax
from jax.experimental import pallas as pl
from jax.experimental.pallas import tpu as pltpu
from jax.sharding import Mesh, PartitionSpec as P

EPSILON = 1e-05
ROWS = 256
TAPS = 128
CHANS = 1024
TOKENS = 32768
CHANNEL_TOTAL = 4096
LANES = 128
TILES = CHANS // LANES
WIDTH = 256
PER = WIDTH // LANES
STEPS = CHANS // WIDTH
GROUPS = TAPS // 8
POINTS = ROWS + TAPS
HALF = POINTS // 2
X, Y, Z, ZL = (4, 4, 16, 4)
ZH = Z // ZL
PLANE = Y * Z
LARGE = 16 * 1024 * 1024
SMALL = 8 * 1024 * 1024
F32 = jnp.float32
BF16 = jnp.bfloat16
DENSE = (TILES, LANES)
FULL = (ROWS, CHANS)


def transform_table():
    k = np.arange(HALF, dtype=np.int64)[:, None]
    n = np.arange(POINTS, dtype=np.int64)[None, :]
    angle = np.pi * (((2 * k + 1) * n) % (2 * POINTS)).astype(np.float64) / POINTS
    table = np.concatenate([np.cos(angle), -np.sin(angle)], axis=0)
    return table.astype(BF16)


ANY = pl.BlockSpec(memory_space=pl.ANY)
VMEM = pl.BlockSpec(memory_space=pltpu.VMEM)


def shape(dims, dtype=F32):
    return jax.ShapeDtypeStruct(dims, dtype)


def cols(ref, step):
    return ref.at[:, pl.ds(step * WIDTH, WIDTH)]


def blocks(ref, step):
    return ref.at[:, pl.ds(step * PER, PER)]


def cost(args, outs, flops):
    sizes = [a.size * a.dtype.itemsize for a in args]
    sizes += [int(np.prod(o.shape)) * o.dtype.itemsize for o in outs]
    return pl.CostEstimate(flops=flops, bytes_accessed=sum(sizes), transcendentals=0)


def small(kernel, outs, *args, specs=None):
    return pl.pallas_call(
        kernel,
        out_shape=tuple(outs),
        in_specs=[VMEM] * len(args) if specs is None else specs,
        out_specs=tuple([VMEM] * len(outs)),
        compiler_params=pltpu.CompilerParams(vmem_limit_bytes=SMALL),
        cost_estimate=cost(args, outs, 0),
    )(*args)


def large(kernel, outs, out_cuts, args, in_cuts, scratch=(), flops=0, grant=LARGE):
    cuts = list(in_cuts) + list(out_cuts)

    def stepped(*refs):
        arrays, extra = (refs[: len(cuts)], refs[len(cuts) :])
        for step in range(STEPS):
            views = [cut(ref, step) if cut in (cols, blocks) else ref for cut, ref in zip(cuts, arrays)]
            kernel(step, *views, *extra)

    specs = [VMEM if cut in (cols, blocks, None) else cut for cut in cuts]
    return pl.pallas_call(
        stepped,
        out_shape=tuple(outs),
        in_specs=specs[: len(args)],
        out_specs=tuple(specs[len(args) :]),
        scratch_shapes=list(scratch),
        compiler_params=pltpu.CompilerParams(vmem_limit_bytes=grant),
        cost_estimate=pl.CostEstimate(flops=flops, bytes_accessed=1024, transcendentals=0),
    )(*args)


def dot(a, b):
    return lax.dot_general(
        a, b, (((1,), (0,)), ((), ())), preferred_element_type=F32
    )


def dot_back(table, b):
    return lax.dot_general(
        table, b, (((0,), (0,)), ((), ())), preferred_element_type=F32
    )


def row(ref, step):
    at = step * PER
    return jnp.concatenate([ref[at + i : at + i + 1, :] for i in range(PER)], axis=1)


def put_row(ref, step, value):
    at = step * PER
    for i in range(PER):
        ref[at + i : at + i + 1, :] = value[:, i * LANES : (i + 1) * LANES]


def fold(value):
    return sum(value[:, i * LANES : (i + 1) * LANES] for i in range(PER))


def row_mean(total_ref):
    packed = total_ref[...] / CHANNEL_TOTAL
    return jnp.concatenate(
        [jnp.broadcast_to(packed[i : i + 1], (LANES, LANES)).T for i in range(ROWS // LANES)], axis=0
    )


def widen(value):
    return jnp.concatenate([value] * PER, axis=1)


def pack_rows(acc, out_ref):
    total = jnp.sum(acc.T, axis=0, keepdims=True)
    out_ref[...] = jnp.concatenate([total[:, :LANES], total[:, LANES:]], axis=0)


def squares_kernel(step, stream_ref, squares_ref, acc_ref):
    value = stream_ref[...].astype(F32)
    squares = fold(value * value)
    acc_ref[...] = squares if step == 0 else acc_ref[...] + squares
    if step == STEPS - 1:
        pack_rows(acc_ref[...], squares_ref)


def scan_kernel(step, out_ref, cot_ref, rate_ref, spread_ref, local_ref, first_ref):
    rank = lax.broadcasted_iota(jnp.int32, (8, WIDTH), 0)
    rate = row(rate_ref, step)
    source = out_ref[...].astype(F32) * cot_ref[...].astype(F32)
    coefs = [(s, jnp.where(rank < 8 - s, jnp.exp(-float(s) * rate), 0.0)) for s in (1, 2, 4)]
    power = jnp.exp(-rate * (8 - rank).astype(F32))
    carry = jnp.zeros((1, WIDTH), F32)
    for group in range(ROWS // 8 - 1, -1, -1):
        value = source[group * 8 : group * 8 + 8, :]
        for s, coef in coefs:
            value = value + coef * pltpu.roll(value, 8 - s, 0)
        value = value + power * carry
        local_ref[group * 8 : group * 8 + 8, :] = value
        carry = value[0:1, :]
    put_row(first_ref, step, carry)
    if step == STEPS - 1:
        spread_ref[...] = jnp.broadcast_to(first_ref[...], spread_ref.shape)


def column_kernel(parts_ref, rate_ref, after_ref, out_ref):
    z = lax.axis_index(("zh", "zl"))
    pace = rate_ref[...] * (-2.0 * ROWS)
    ahead = jnp.zeros(DENSE, F32)
    total = jnp.zeros(DENSE, F32)
    for other in range(Z):
        value = parts_ref[other]
        gap = other - z - 1
        weight = jnp.exp(pace * jnp.maximum(gap, 0).astype(F32))
        ahead = ahead + jnp.where(gap >= 0, weight, 0.0) * value
        total = total + jnp.exp(pace * float(other)) * value
    count = out_ref.shape[0]
    out_ref[:, 0] = jnp.broadcast_to(total, (count,) + DENSE)
    out_ref[:, 1] = jnp.broadcast_to(ahead, (count,) + DENSE)
    out_ref[:, 2] = jnp.broadcast_to(parts_ref[z], (count,) + DENSE)


def find_carry(parts_ref, rate_ref, carry_ref):
    y, z, core = (lax.axis_index("y"), lax.axis_index(("zh", "zl")), lax.axis_index("core"))
    rate = rate_ref[...]
    decay = jnp.exp(-ROWS * rate)
    rest = jnp.exp(rate * (-2.0 * ROWS) * (Z - 1 - z).astype(F32))
    both = []
    for parity in range(2):
        planes = jnp.zeros(DENSE, F32)
        for later in range(1, Y):
            gap = later - y - 1
            weight = jnp.exp(rate * (-2.0 * ROWS * Z) * jnp.maximum(gap, 0).astype(F32))
            planes = planes + jnp.where(gap >= 0, weight, 0.0) * parts_ref[later * 2 + parity, 0]
        both.append(parts_ref[y * 2 + parity, 1] + rest * planes)
    last = both[0] + decay * both[1]
    carry_ref[...] = jnp.where(core == 0, parts_ref[y * 2 + 1, 2] + decay * last, last)


def product_kernel(step, after_ref, total_ref, stream_ref, key_ref, gain_ref, product_ref, rim_ref, inv_ref):
    if step == 0:
        inv_ref[...] = lax.rsqrt(row_mean(total_ref) + EPSILON)

    normed = stream_ref[...].astype(F32) * widen(inv_ref[...]) * row(gain_ref, step)
    product = key_ref[...].astype(F32) * normed
    product_ref[...] = product.astype(BF16)
    rim_ref[...] = product[ROWS - TAPS :, :]


def mul_conj(a, b):
    ar, ai = (a[:HALF], a[HALF:])
    br, bi = (b[:HALF], b[HALF:])
    return jnp.concatenate([ar * br + ai * bi, ar * bi - ai * br], axis=0).astype(BF16)


def mul(a, b):
    ar, ai = (a[:HALF], a[HALF:])
    br, bi = (b[:HALF], b[HALF:])
    return jnp.concatenate([ar * br - ai * bi, ar * bi + ai * br], axis=0).astype(BF16)


def grad_stored(step, local_ref, rate_ref, scale_ref, carry_ref):
    rate = row(rate_ref, step)
    rank = lax.broadcasted_iota(jnp.int32, (8, WIDTH), 0)
    power = jnp.exp(-rate * (8 - rank).astype(F32)) * row(carry_ref, step)
    groups = []
    for group in range(ROWS // 8):
        far = power * jnp.exp(-rate * float(ROWS - 8 - 8 * group))
        groups.append(local_ref[group * 8 : group * 8 + 8, :] + far)
    return jnp.concatenate(groups, axis=0) * row(scale_ref, step)


def filter_kernel(
    step, fwd_ref, product_ref, rim_ref, local_ref, query_ref, rate_ref, scale_ref, sums_ref,
    keep_ref, send_ref, mixed_grad_ref, head_ref, carry_ref,
):
    if step == 0:
        find_carry(sums_ref, rate_ref, carry_ref)
    ext = jnp.concatenate([rim_ref[...].astype(BF16), product_ref[...]], axis=0)
    product = dot(fwd_ref[...], ext)
    grad_mixed = query_ref[...].astype(F32) * grad_stored(step, local_ref, rate_ref, scale_ref, carry_ref)
    head_ref[...] = grad_mixed[:TAPS]
    grad_mixed = grad_mixed.astype(BF16)
    mixed_grad_ref[...] = grad_mixed
    spectrum = dot(fwd_ref[:, :ROWS], grad_mixed)
    taps = -dot_back(fwd_ref[:, ROWS:], mul_conj(product, spectrum))
    is_first = lax.axis_index("core") == 0
    for group in range(GROUPS // 2):
        low = taps[group * 8 : group * 8 + 8, :]
        high = taps[TAPS // 2 + group * 8 : TAPS // 2 + group * 8 + 8, :]
        keep = jnp.where(is_first, low, high)
        send = jnp.where(is_first, high, low)
        for i in range(PER):
            keep_ref[group, i] = keep[:, i * LANES : (i + 1) * LANES]
            send_ref[group, i] = send[:, i * LANES : (i + 1) * LANES]


def query_kernel(
    step, fwd_ref, product_ref, rim_ref, local_ref, filter_ref, rate_ref, scale_ref, carry_ref, grad_ref, token_ref
):
    ext = jnp.concatenate([rim_ref[...].astype(BF16), product_ref[...]], axis=0)
    product = dot(fwd_ref[...], ext)
    taps = dot(fwd_ref[:, :TAPS], filter_ref[...].astype(BF16))
    mixed = dot_back(fwd_ref[:, TAPS:], mul(product, taps)) * (2.0 / POINTS)
    grad_ref[...] = (mixed * grad_stored(step, local_ref, rate_ref, scale_ref, carry_ref)).astype(BF16)
    if step == STEPS - 1:
        token_ref[...] = carry_ref[...]


def weighted_kernel(
    step, later_ref, fwd_ref, grad_ref, after_ref, filter_ref, key_ref, stream_ref, gain_ref, weighted_ref, dots_ref, acc_ref
):
    ext = jnp.concatenate([grad_ref[...], after_ref[...].astype(BF16)], axis=0)
    grad = dot(fwd_ref[...], ext)
    taps = dot(fwd_ref[:, :TAPS], filter_ref[...].astype(BF16))
    back = dot_back(fwd_ref[:, :ROWS], mul_conj(taps, grad)) * (2.0 / POINTS)
    weighted = row(gain_ref, step) * key_ref[...].astype(F32) * back
    weighted_ref[...] = weighted
    dots = fold(weighted * stream_ref[...].astype(F32))

    if step == 0:
        acc_ref[...] = dots
    else:
        acc_ref[...] += dots

    if step == STEPS - 1:
        pack_rows(acc_ref[...], dots_ref)


def stream_kernel(step, total_ref, dots_ref, weighted_ref, stream_ref, out_ref, inv_ref, factor_ref):
    if step == 0:
        inv_ref[...] = lax.rsqrt(row_mean(total_ref) + EPSILON)
        factor_ref[...] = inv_ref[...] * inv_ref[...] * row_mean(dots_ref)

    value = weighted_ref[...] - stream_ref[...].astype(F32) * widen(factor_ref[...])
    out_ref[...] = (widen(inv_ref[...]) * value).astype(BF16)


def gate_kernel(value_ref, after_ref, out_ref):
    out_ref[...] = value_ref[...]


def add_kernel(a_ref, b_ref, out_ref):
    out_ref[...] = a_ref[...] + b_ref[...]


def spread_sum_kernel(parts_ref, *refs):
    spread_ref = refs[-1]
    total = jnp.sum(parts_ref[...], axis=0)
    spread_ref[...] = jnp.broadcast_to(total, spread_ref.shape)


def finish_kernel(own_ref, other_ref, filter_ref, residue_ref, filter_out, residue_out):
    scale = TOKENS ** (-0.5) * 2.0 / POINTS
    count = own_ref.shape[0]
    is_first = lax.axis_index("core") == 0
    for tile in range(TILES):
        lanes = slice(tile * LANES, (tile + 1) * LANES)
        total = jnp.zeros((8, LANES), F32)
        for group in range(GROUPS):
            at = (group * TILES + tile) % count
            low = group * TILES + tile < count
            own, other = (own_ref[at], other_ref[at])
            value = jnp.where(is_first, own, other) if low else jnp.where(is_first, other, own)
            value = value * scale
            rows = slice(group * 8, group * 8 + 8)
            filter_out[rows, lanes] = value
            total = total + filter_ref[rows, lanes] * value
        total = jnp.sum(total, axis=0, keepdims=True)
        residue_out[tile : tile + 1, :] = total / residue_ref[tile : tile + 1, :]


def body(
    stream, norm_gain, gate_query, gate_key, gate_out, cotangent, medium_filter, long_residue, long_rate
):
    forward = jnp.asarray(transform_table())
    gain, rate, residue = (v.reshape(DENSE) for v in (norm_gain, long_rate, long_residue))
    scale = residue * jnp.sqrt(-jnp.expm1(-2.0 * rate))
    swap = [(0, 1), (1, 0)]
    seq = ("y", "zh", "zl", "core")
    count = 2 * PLANE

    packed = (ROWS // LANES, LANES)
    spread, local = large(
        scan_kernel, [shape((Z,) + DENSE), shape(FULL)], [None, cols], (gate_out, cotangent, rate),
        [cols, cols, None], scratch=[pltpu.VMEM(DENSE, F32)], grant=60 * 1024 * 1024,
    )
    column = lax.all_to_all(spread, ("zh", "zl"), 0, 0, tiled=True)
    (squares,) = large(
        squares_kernel, [shape(packed)], [None], (stream,), [cols], scratch=[pltpu.VMEM((ROWS, LANES), F32)]
    )
    squares = lax.psum(squares, "chan")
    product, rim = large(
        product_kernel, [shape(FULL, BF16), shape((TAPS, CHANS))], [cols, cols],
        (column, squares, stream, gate_key, gain), [None, None, cols, cols, None],
        scratch=[pltpu.VMEM((ROWS, LANES), F32)],
    )
    before = lax.ppermute(rim, seq, [(i, i + 1) for i in range(count - 1)])
    (sums,) = small(
        column_kernel, [shape((2 * Y, 3) + DENSE)], column, rate, scale
    )
    sums = lax.all_to_all(sums, ("y", "core"), 0, 0, tiled=True)

    half = (GROUPS // 2, TILES, 8, LANES)
    keep, send, grad_mixed, head, carry = large(
        filter_kernel, [shape(half), shape(half), shape(FULL, BF16), shape((TAPS, CHANS)), shape(DENSE)],
        [blocks, blocks, cols, cols, None],
        (forward, product, before, local, gate_query, rate, scale, sums),
        [None, cols, cols, cols, cols, None, None, None],
        flops=2 * CHANS * POINTS * (POINTS + ROWS + TAPS),
    )

    got = lax.ppermute(send, "core", swap)
    (chip_sum,) = small(add_kernel, [shape(half)], keep, got)
    after = lax.ppermute(head, seq, [(i + 1, i) for i in range(count - 1)])
    parts = lax.all_to_all(chip_sum.reshape(PLANE, 8, LANES), ("y", "zl"), 0, 0, tiled=True)
    grad_query, token = large(
        query_kernel, [shape(FULL, BF16), shape(DENSE)], [cols, None],
        (forward, product, before, local, medium_filter, rate, scale, carry),
        [None, cols, cols, cols, cols, None, None, None],
        flops=2 * CHANS * POINTS * (POINTS + ROWS + TAPS),
    )
    mine = (ZH, 8, LANES)
    (spread,) = small(
        spread_sum_kernel, [shape((ZH,) + mine)], parts.reshape((Y * ZL,) + mine), token, specs=[VMEM, ANY]
    )
    parts = lax.all_to_all(spread, "zh", 0, 0, tiled=True)
    weighted, dots = large(
        weighted_kernel, [shape(FULL), shape(packed)], [cols, None],
        (spread, forward, grad_mixed, after, medium_filter, gate_key, stream, gain),
        [ANY, None, cols, cols, cols, cols, cols, None],
        scratch=[pltpu.VMEM((ROWS, LANES), F32)],
        flops=2 * CHANS * POINTS * (POINTS + ROWS + TAPS),
    )
    (spread,) = small(
        spread_sum_kernel, [shape((Y * ZL,) + mine)], parts, dots, specs=[VMEM, ANY]
    )
    dots = lax.psum(dots, "chan")
    own_half = lax.all_to_all(spread, ("y", "zl"), 0, 0, tiled=True).reshape(PLANE, 8, LANES)
    (grad_stream,) = large(
        stream_kernel, [shape(FULL, BF16)], [cols],
        (squares, dots, weighted, stream), [None, None] + [cols] * 2,
        scratch=[pltpu.VMEM((ROWS, LANES), F32)] * 2,
    )
    (own_half,) = small(gate_kernel, [shape(own_half.shape)], own_half, dots, specs=[VMEM, ANY])
    other_half = lax.ppermute(own_half, "core", swap)
    grad_filter, grad_residue = small(
        finish_kernel, [shape((TAPS, CHANS)), shape(DENSE)], own_half, other_half, medium_filter,
        residue,
    )
    return (grad_query, grad_stream, grad_filter, grad_residue.reshape(CHANS))


def solution(mesh):
    devices = mesh.devices.reshape(Y, ZH, ZL, 2, mesh.devices.shape[1])
    fine = Mesh(devices, ("y", "zh", "zl", "core", "chan"))
    seq = ("y", "zh", "zl", "core")
    rows, chans = (P(seq, "chan"), P("chan"))
    in_specs = (rows, chans, rows, rows, rows, rows, P(None, "chan"), chans, chans)
    out_specs = (rows, rows, P(None, "chan"), chans)
    return jax.shard_map(body, mesh=fine, in_specs=in_specs, out_specs=out_specs, check_vma=False)
```

```python
import jax
import jax.numpy as jnp
import numpy as np
from jax import lax
from jax.experimental import pallas as pl
from jax.experimental.pallas import tpu as pltpu
from jax.sharding import Mesh, PartitionSpec as P

EPSILON = 1e-05
ROWS = 256
TAPS = 128
CHANS = 1024
TOKENS = 32768
CHANNEL_TOTAL = 4096
LANES = 128
TILES = CHANS // LANES
WIDTH = 256
PER = WIDTH // LANES
STEPS = CHANS // WIDTH
GROUPS = TAPS // 8
POINTS = ROWS + TAPS
HALF = POINTS // 2
X, Y, Z, ZL = (4, 4, 16, 4)
ZH = Z // ZL
PLANE = Y * Z
LARGE = 16 * 1024 * 1024
SMALL = 8 * 1024 * 1024
F32 = jnp.float32
BF16 = jnp.bfloat16
DENSE = (TILES, LANES)
FULL = (ROWS, CHANS)


def transform_table():
    k = np.arange(HALF, dtype=np.int64)[:, None]
    n = np.arange(POINTS, dtype=np.int64)[None, :]
    angle = np.pi * (((2 * k + 1) * n) % (2 * POINTS)).astype(np.float64) / POINTS
    table = np.concatenate([np.cos(angle), -np.sin(angle)], axis=0)
    return table.astype(BF16)


ANY = pl.BlockSpec(memory_space=pl.ANY)
VMEM = pl.BlockSpec(memory_space=pltpu.VMEM)


def shape(dims, dtype=F32):
    return jax.ShapeDtypeStruct(dims, dtype)


def cols(ref, step):
    return ref.at[:, pl.ds(step * WIDTH, WIDTH)]


def blocks(ref, step):
    return ref.at[:, pl.ds(step * PER, PER)]


def cost(args, outs, flops):
    sizes = [a.size * a.dtype.itemsize for a in args]
    sizes += [int(np.prod(o.shape)) * o.dtype.itemsize for o in outs]
    return pl.CostEstimate(flops=flops, bytes_accessed=sum(sizes), transcendentals=0)


def small(kernel, outs, *args, specs=None):
    return pl.pallas_call(
        kernel,
        out_shape=tuple(outs),
        in_specs=[VMEM] * len(args) if specs is None else specs,
        out_specs=tuple([VMEM] * len(outs)),
        compiler_params=pltpu.CompilerParams(vmem_limit_bytes=SMALL),
        cost_estimate=cost(args, outs, 0),
    )(*args)


def large(kernel, outs, out_cuts, args, in_cuts, scratch=(), flops=0, grant=LARGE):
    cuts = list(in_cuts) + list(out_cuts)

    def stepped(*refs):
        arrays, extra = (refs[: len(cuts)], refs[len(cuts) :])
        for step in range(STEPS):
            views = [cut(ref, step) if cut in (cols, blocks) else ref for cut, ref in zip(cuts, arrays)]
            kernel(step, *views, *extra)

    specs = [VMEM if cut in (cols, blocks, None) else cut for cut in cuts]
    return pl.pallas_call(
        stepped,
        out_shape=tuple(outs),
        in_specs=specs[: len(args)],
        out_specs=tuple(specs[len(args) :]),
        scratch_shapes=list(scratch),
        compiler_params=pltpu.CompilerParams(vmem_limit_bytes=grant),
        cost_estimate=pl.CostEstimate(flops=flops, bytes_accessed=1024, transcendentals=0),
    )(*args)


def dot(a, b):
    return lax.dot_general(
        a, b, (((1,), (0,)), ((), ())), preferred_element_type=F32
    )


def dot_back(table, b):
    return lax.dot_general(
        table, b, (((0,), (0,)), ((), ())), preferred_element_type=F32
    )


def row(ref, step):
    at = step * PER
    return jnp.concatenate([ref[at + i : at + i + 1, :] for i in range(PER)], axis=1)


def put_row(ref, step, value):
    at = step * PER
    for i in range(PER):
        ref[at + i : at + i + 1, :] = value[:, i * LANES : (i + 1) * LANES]


def fold(value):
    return sum(value[:, i * LANES : (i + 1) * LANES] for i in range(PER))


def row_mean(total_ref):
    packed = total_ref[...] / CHANNEL_TOTAL
    return jnp.concatenate(
        [jnp.broadcast_to(packed[i : i + 1], (LANES, LANES)).T for i in range(ROWS // LANES)], axis=0
    )


def widen(value):
    return jnp.concatenate([value] * PER, axis=1)


def pack_rows(acc, out_ref):
    total = jnp.sum(acc.T, axis=0, keepdims=True)
    out_ref[...] = jnp.concatenate([total[:, :LANES], total[:, LANES:]], axis=0)


def squares_kernel(step, stream_ref, squares_ref, acc_ref):
    value = stream_ref[...].astype(F32)
    squares = fold(value * value)
    acc_ref[...] = squares if step == 0 else acc_ref[...] + squares
    if step == STEPS - 1:
        pack_rows(acc_ref[...], squares_ref)


def scan_kernel(step, out_ref, cot_ref, rate_ref, spread_ref, local_ref, first_ref):
    rank = lax.broadcasted_iota(jnp.int32, (8, WIDTH), 0)
    rate = row(rate_ref, step)
    source = out_ref[...].astype(F32) * cot_ref[...].astype(F32)
    coefs = [(s, jnp.where(rank < 8 - s, jnp.exp(-float(s) * rate), 0.0)) for s in (1, 2, 4)]
    power = jnp.exp(-rate * (8 - rank).astype(F32))
    carry = jnp.zeros((1, WIDTH), F32)
    for group in range(ROWS // 8 - 1, -1, -1):
        value = source[group * 8 : group * 8 + 8, :]
        for s, coef in coefs:
            value = value + coef * pltpu.roll(value, 8 - s, 0)
        value = value + power * carry
        local_ref[group * 8 : group * 8 + 8, :] = value
        carry = value[0:1, :]
    put_row(first_ref, step, carry)
    if step == STEPS - 1:
        spread_ref[...] = jnp.broadcast_to(first_ref[...], spread_ref.shape)


def column_kernel(parts_ref, rate_ref, after_ref, out_ref):
    z = lax.axis_index(("zh", "zl"))
    pace = rate_ref[...] * (-2.0 * ROWS)
    ahead = jnp.zeros(DENSE, F32)
    total = jnp.zeros(DENSE, F32)
    for other in range(Z):
        value = parts_ref[other]
        gap = other - z - 1
        weight = jnp.exp(pace * jnp.maximum(gap, 0).astype(F32))
        ahead = ahead + jnp.where(gap >= 0, weight, 0.0) * value
        total = total + jnp.exp(pace * float(other)) * value
    count = out_ref.shape[0]
    out_ref[:, 0] = jnp.broadcast_to(total, (count,) + DENSE)
    out_ref[:, 1] = jnp.broadcast_to(ahead, (count,) + DENSE)
    out_ref[:, 2] = jnp.broadcast_to(parts_ref[z], (count,) + DENSE)


def find_carry(parts_ref, rate_ref, carry_ref):
    y, z, core = (lax.axis_index("y"), lax.axis_index(("zh", "zl")), lax.axis_index("core"))
    rate = rate_ref[...]
    decay = jnp.exp(-ROWS * rate)
    rest = jnp.exp(rate * (-2.0 * ROWS) * (Z - 1 - z).astype(F32))
    both = []
    for parity in range(2):
        planes = jnp.zeros(DENSE, F32)
        for later in range(1, Y):
            gap = later - y - 1
            weight = jnp.exp(rate * (-2.0 * ROWS * Z) * jnp.maximum(gap, 0).astype(F32))
            planes = planes + jnp.where(gap >= 0, weight, 0.0) * parts_ref[later * 2 + parity, 0]
        both.append(parts_ref[y * 2 + parity, 1] + rest * planes)
    last = both[0] + decay * both[1]
    carry_ref[...] = jnp.where(core == 0, parts_ref[y * 2 + 1, 2] + decay * last, last)


def product_kernel(step, after_ref, total_ref, stream_ref, key_ref, gain_ref, product_ref, rim_ref, inv_ref):
    if step == 0:
        inv_ref[...] = lax.rsqrt(row_mean(total_ref) + EPSILON)

    normed = stream_ref[...].astype(F32) * widen(inv_ref[...]) * row(gain_ref, step)
    product = key_ref[...].astype(F32) * normed
    product_ref[...] = product.astype(BF16)
    rim_ref[...] = product[ROWS - TAPS :, :]


def mul_conj(a, b):
    ar, ai = (a[:HALF], a[HALF:])
    br, bi = (b[:HALF], b[HALF:])
    return jnp.concatenate([ar * br + ai * bi, ar * bi - ai * br], axis=0).astype(BF16)


def mul(a, b):
    ar, ai = (a[:HALF], a[HALF:])
    br, bi = (b[:HALF], b[HALF:])
    return jnp.concatenate([ar * br - ai * bi, ar * bi + ai * br], axis=0).astype(BF16)


def grad_stored(step, local_ref, rate_ref, scale_ref, carry_ref):
    rate = row(rate_ref, step)
    rank = lax.broadcasted_iota(jnp.int32, (8, WIDTH), 0)
    power = jnp.exp(-rate * (8 - rank).astype(F32)) * row(carry_ref, step)
    groups = []
    for group in range(ROWS // 8):
        far = power * jnp.exp(-rate * float(ROWS - 8 - 8 * group))
        groups.append(local_ref[group * 8 : group * 8 + 8, :] + far)
    return jnp.concatenate(groups, axis=0) * row(scale_ref, step)


def filter_kernel(
    step, fwd_ref, product_ref, rim_ref, local_ref, query_ref, rate_ref, scale_ref, sums_ref,
    keep_ref, send_ref, mixed_grad_ref, head_ref, carry_ref, edge_ref,
):
    if step == 0:
        find_carry(sums_ref, rate_ref, carry_ref)
    edge = rim_ref[...].astype(BF16)
    edge_ref[...] = edge
    ext = jnp.concatenate([edge, product_ref[...]], axis=0)
    product = dot(fwd_ref[...], ext)
    grad_mixed = query_ref[...].astype(F32) * grad_stored(step, local_ref, rate_ref, scale_ref, carry_ref)
    head_ref[...] = grad_mixed[:TAPS]
    grad_mixed = grad_mixed.astype(BF16)
    mixed_grad_ref[...] = grad_mixed
    spectrum = dot(fwd_ref[:, :ROWS], grad_mixed)
    taps = -dot_back(fwd_ref[:, ROWS:], mul_conj(product, spectrum))
    is_first = lax.axis_index("core") == 0
    for group in range(GROUPS // 2):
        low = taps[group * 8 : group * 8 + 8, :]
        high = taps[TAPS // 2 + group * 8 : TAPS // 2 + group * 8 + 8, :]
        keep = jnp.where(is_first, low, high)
        send = jnp.where(is_first, high, low)
        for i in range(PER):
            keep_ref[group, i] = keep[:, i * LANES : (i + 1) * LANES]
            send_ref[group, i] = send[:, i * LANES : (i + 1) * LANES]


def query_kernel(
    step, fwd_ref, product_ref, edge_ref, local_ref, filter_ref, rate_ref, scale_ref, carry_ref, grad_ref, token_ref
):
    ext = jnp.concatenate([edge_ref[...], product_ref[...]], axis=0)
    product = dot(fwd_ref[...], ext)
    taps = dot(fwd_ref[:, :TAPS], filter_ref[...].astype(BF16))
    mixed = dot_back(fwd_ref[:, TAPS:], mul(product, taps)) * (2.0 / POINTS)
    grad_ref[...] = (mixed * grad_stored(step, local_ref, rate_ref, scale_ref, carry_ref)).astype(BF16)
    if step == STEPS - 1:
        token_ref[...] = carry_ref[...]


def weighted_kernel(
    step, later_ref, fwd_ref, grad_ref, after_ref, filter_ref, key_ref, stream_ref, gain_ref, weighted_ref, dots_ref, acc_ref
):
    ext = jnp.concatenate([grad_ref[...], after_ref[...].astype(BF16)], axis=0)
    grad = dot(fwd_ref[...], ext)
    taps = dot(fwd_ref[:, :TAPS], filter_ref[...].astype(BF16))
    back = dot_back(fwd_ref[:, :ROWS], mul_conj(taps, grad)) * (2.0 / POINTS)
    weighted = row(gain_ref, step) * key_ref[...].astype(F32) * back
    weighted_ref[...] = weighted
    dots = fold(weighted * stream_ref[...].astype(F32))

    if step == 0:
        acc_ref[...] = dots
    else:
        acc_ref[...] += dots

    if step == STEPS - 1:
        pack_rows(acc_ref[...], dots_ref)


def stream_kernel(step, total_ref, dots_ref, weighted_ref, stream_ref, out_ref, inv_ref, factor_ref):
    if step == 0:
        inv_ref[...] = lax.rsqrt(row_mean(total_ref) + EPSILON)
        factor_ref[...] = inv_ref[...] * inv_ref[...] * row_mean(dots_ref)

    value = weighted_ref[...] - stream_ref[...].astype(F32) * widen(factor_ref[...])
    out_ref[...] = (widen(inv_ref[...]) * value).astype(BF16)


def gate_kernel(value_ref, after_ref, out_ref):
    out_ref[...] = value_ref[...]


def add_kernel(a_ref, b_ref, out_ref):
    out_ref[...] = a_ref[...] + b_ref[...]


def spread_sum_kernel(parts_ref, *refs):
    spread_ref = refs[-1]
    total = jnp.sum(parts_ref[...], axis=0)
    spread_ref[...] = jnp.broadcast_to(total, spread_ref.shape)


def finish_kernel(own_ref, other_ref, filter_ref, residue_ref, filter_out, residue_out):
    scale = TOKENS ** (-0.5) * 2.0 / POINTS
    count = own_ref.shape[0]
    is_first = lax.axis_index("core") == 0
    for tile in range(TILES):
        lanes = slice(tile * LANES, (tile + 1) * LANES)
        total = jnp.zeros((8, LANES), F32)
        for group in range(GROUPS):
            at = (group * TILES + tile) % count
            low = group * TILES + tile < count
            own, other = (own_ref[at], other_ref[at])
            value = jnp.where(is_first, own, other) if low else jnp.where(is_first, other, own)
            value = value * scale
            rows = slice(group * 8, group * 8 + 8)
            filter_out[rows, lanes] = value
            total = total + filter_ref[rows, lanes] * value
        total = jnp.sum(total, axis=0, keepdims=True)
        residue_out[tile : tile + 1, :] = total / residue_ref[tile : tile + 1, :]


def body(
    stream, norm_gain, gate_query, gate_key, gate_out, cotangent, medium_filter, long_residue, long_rate
):
    forward = jnp.asarray(transform_table())
    gain, rate, residue = (v.reshape(DENSE) for v in (norm_gain, long_rate, long_residue))
    scale = residue * jnp.sqrt(-jnp.expm1(-2.0 * rate))
    swap = [(0, 1), (1, 0)]
    seq = ("y", "zh", "zl", "core")
    count = 2 * PLANE

    packed = (ROWS // LANES, LANES)
    spread, local = large(
        scan_kernel, [shape((Z,) + DENSE), shape(FULL)], [None, cols], (gate_out, cotangent, rate),
        [cols, cols, None], scratch=[pltpu.VMEM(DENSE, F32)], grant=60 * 1024 * 1024,
    )
    column = lax.all_to_all(spread, ("zh", "zl"), 0, 0, tiled=True)
    (squares,) = large(
        squares_kernel, [shape(packed)], [None], (stream,), [cols], scratch=[pltpu.VMEM((ROWS, LANES), F32)]
    )
    squares = lax.psum(squares, "chan")
    product, rim = large(
        product_kernel, [shape(FULL, BF16), shape((TAPS, CHANS))], [cols, cols],
        (column, squares, stream, gate_key, gain), [None, None, cols, cols, None],
        scratch=[pltpu.VMEM((ROWS, LANES), F32)],
    )
    before = lax.ppermute(rim, seq, [(i, i + 1) for i in range(count - 1)])
    (sums,) = small(
        column_kernel, [shape((2 * Y, 3) + DENSE)], column, rate, scale
    )
    sums = lax.all_to_all(sums, ("y", "core"), 0, 0, tiled=True)

    half = (GROUPS // 2, TILES, 8, LANES)
    keep, send, grad_mixed, head, carry, edge = large(
        filter_kernel, [shape(half), shape(half), shape(FULL, BF16), shape((TAPS, CHANS)), shape(DENSE),
         shape((TAPS, CHANS), BF16)],
        [blocks, blocks, cols, cols, None, cols],
        (forward, product, before, local, gate_query, rate, scale, sums),
        [None, cols, cols, cols, cols, None, None, None],
        flops=2 * CHANS * POINTS * (POINTS + ROWS + TAPS),
    )

    got = lax.ppermute(send, "core", swap)
    (chip_sum,) = small(add_kernel, [shape(half)], keep, got)
    after = lax.ppermute(head, seq, [(i + 1, i) for i in range(count - 1)])
    parts = lax.all_to_all(chip_sum.reshape(PLANE, 8, LANES), ("y", "zl"), 0, 0, tiled=True)
    grad_query, token = large(
        query_kernel, [shape(FULL, BF16), shape(DENSE)], [cols, None],
        (forward, product, edge, local, medium_filter, rate, scale, carry),
        [None, cols, cols, cols, cols, None, None, None],
        flops=2 * CHANS * POINTS * (POINTS + ROWS + TAPS),
    )
    mine = (ZH, 8, LANES)
    (spread,) = small(
        spread_sum_kernel, [shape((ZH,) + mine)], parts.reshape((Y * ZL,) + mine), token, specs=[VMEM, ANY]
    )
    parts = lax.all_to_all(spread, "zh", 0, 0, tiled=True)
    weighted, dots = large(
        weighted_kernel, [shape(FULL), shape(packed)], [cols, None],
        (spread, forward, grad_mixed, after, medium_filter, gate_key, stream, gain),
        [ANY, None, cols, cols, cols, cols, cols, None],
        scratch=[pltpu.VMEM((ROWS, LANES), F32)],
        flops=2 * CHANS * POINTS * (POINTS + ROWS + TAPS),
    )
    (spread,) = small(
        spread_sum_kernel, [shape((Y * ZL,) + mine)], parts, dots, specs=[VMEM, ANY]
    )
    dots = lax.psum(dots, "chan")
    own_half = lax.all_to_all(spread, ("y", "zl"), 0, 0, tiled=True).reshape(PLANE, 8, LANES)
    (grad_stream,) = large(
        stream_kernel, [shape(FULL, BF16)], [cols],
        (squares, dots, weighted, stream), [None, None] + [cols] * 2,
        scratch=[pltpu.VMEM((ROWS, LANES), F32)] * 2,
    )
    (own_half,) = small(gate_kernel, [shape(own_half.shape)], own_half, dots, specs=[VMEM, ANY])
    other_half = lax.ppermute(own_half, "core", swap)
    grad_filter, grad_residue = small(
        finish_kernel, [shape((TAPS, CHANS)), shape(DENSE)], own_half, other_half, medium_filter,
        residue,
    )
    return (grad_query, grad_stream, grad_filter, grad_residue.reshape(CHANS))


def solution(mesh):
    devices = mesh.devices.reshape(Y, ZH, ZL, 2, mesh.devices.shape[1])
    fine = Mesh(devices, ("y", "zh", "zl", "core", "chan"))
    seq = ("y", "zh", "zl", "core")
    rows, chans = (P(seq, "chan"), P("chan"))
    in_specs = (rows, chans, rows, rows, rows, rows, P(None, "chan"), chans, chans)
    out_specs = (rows, rows, P(None, "chan"), chans)
    return jax.shard_map(body, mesh=fine, in_specs=in_specs, out_specs=out_specs, check_vma=False)
```
